256 devices in a mesh: segment: 4 (over y), rows: 64 (over x, z, core).
Axes of the slice: x: 4, y: 4, z: 8, core: 2. Of those that a mesh axis runs over, the one named last changes fastest.
Arguments:
- hidden_in: bfloat16 [4096, 8192], P('rows'), may hold values from -6 to 6
- request_adapter: int32 [4096, 1], P('rows'), may hold values from 0 to 63; in each aligned block of 64 rows (0 to 63, 64 to 127, ...) at most 2 rows name the same one
- home_slot: int32 [64], replicated, may hold values from 0 to 63, each once
- gains: float32 [4, 8192], P('segment'), may hold values from 0.5 to 1.5
- shrink_tiles: bfloat16 [4, 64, 8192, 64], P('segment', 'rows'), may hold values from -0.0625 to 0.0625
- expand_tiles: bfloat16 [4, 64, 64, 8192], P('segment', 'rows'), may hold values from -0.75 to 0.75
Outputs:
- section_out: bfloat16 [4, 4096, 8192], P('segment', 'rows')
The draws below stay inside these ranges and needn't reach their ends.
Inputs may be any that keep to these rules, and one draw needn't show every extreme that they name: `request_adapter`: no adapter is used by more than 2 requests of one index of rows (the requests of one device); some adapter is used by exactly 2 of them. Every adapter is used by some request. A permutation: adapter a's factors stand at index home_slot[a] of the adapter dimension of shrink_tiles and expand_tiles.
All inputs are finite; a program needn't handle non-finite values.
Results may differ from the reference program's by a relative error of at most 0.0095.
Values may be sent and summed in bfloat16 or wider, within the bound.
No kernel may reach another device: no remote copies, remote signals or barrier semaphores. Data moves between devices by JAX's collectives and lax.ppermute only.
A program may use at most 64 MiB of HBM per device.

```python
import math
import jax
import jax.numpy as jnp
import numpy as np
from jax import lax

D = 8192
RANK = 64
REQ_DEV = 64
ADAPTERS = 64
MOST = 2
TOKENS = 4096
N_SEGMENT = 4
N_ROWS = 64


def block_levels(rng, extent, shards, low, top_value):
    level = 1.0
    for position, shards_of in shards:
        draws = jax.random.uniform(jax.random.fold_in(jax.random.fold_in(rng, 6), position), (shards_of,), jnp.float32, low / len(shards), top_value / len(shards))
        level = level * jnp.repeat(jnp.exp(draws), extent[position] // shards_of).reshape((-1,) + (1,) * (len(extent) - 1 - position))
    return level


def assign_block(stream_key, own, number, rows, amount, top, limit, skew):
    ranking = jax.random.permutation(stream_key, amount)
    packed, usual = portions_of(amount, rows * top, limit, skew, True), portions_of(amount, rows * top, limit, skew, False)
    places = jnp.arange(amount)

    def named(lengths, rotation):
        used = int((lengths > 0).sum())
        fixed = max(1, used // 4)
        passed = fixed + (places - fixed + rotation * (used - fixed)) % max(1, amount - fixed)
        return jnp.zeros((amount,), jnp.int32).at[ranking[jnp.where(places < fixed, places, passed)]].set(jnp.asarray(lengths, jnp.int32))

    lengths = jnp.where(number % 4 == 0, named(packed, number // 4), named(usual, number - number // 4 - 1))
    mixed = jax.random.permutation(jax.random.fold_in(own, 3), amount)
    giver, sink = mixed[0:amount // 2 * 2:2], mixed[1:amount // 2 * 2:2]
    margin = jnp.minimum(lengths[giver] - 1, limit - lengths[sink]) // 2
    margin = jnp.where((giver == ranking[0]) | (sink == ranking[0]) | (lengths[sink] == 0), 0, jnp.maximum(margin, 0))
    passed = jax.random.randint(jax.random.fold_in(own, 4), (amount // 2,), 0, 1 << 20) % (margin + 1)
    lengths = lengths.at[giver].add(-passed).at[sink].add(passed)
    labels = jnp.searchsorted(jnp.cumsum(lengths), jnp.arange(rows * top), side="right").astype(jnp.int32)
    grid = labels.reshape(top, rows).T
    grid = grid[jax.random.permutation(jax.random.fold_in(own, 1), rows)]
    rotation = jax.random.randint(jax.random.fold_in(own, 2), (rows, 1), 0, top)
    return jnp.take_along_axis(grid, (jnp.arange(top)[None, :] + rotation) % top, axis=1)


def portions_of(number_of, total, bound, slope, full):
    loads = [(1 << 20) // math.isqrt(standing ** slope) + 1 for standing in range(1, number_of + 1)]
    largest = bound if full else min(bound, max(-(-total // number_of), total * loads[0] // sum(loads)))
    least = 1 if total - largest >= number_of - 1 else 0
    given, spare = [largest] + [least] * (number_of - 1), total - largest - least * (number_of - 1)
    while spare > 0:
        candidates = [i for i in range(1, number_of) if given[i] < largest] or [i for i in range(1, number_of) if given[i] < bound]
        mass, remaining = sum([loads[i] for i in candidates]), spare
        for i in candidates:
            more = min(bound - given[i], max(1, remaining * loads[i] // mass), spare)
            given[i] = given[i] + more
            spare = spare - more
    return np.array(given)


def normal_values(own_key, extent, scale, bound, pieces=(), dtype=jnp.bfloat16):
    values = scale * jax.random.normal(own_key, extent, jnp.float32)
    if pieces:
        values = values * block_levels(own_key, extent, pieces, -0.22, 0.18)
    return jnp.clip(values, -bound, bound).astype(dtype)


def setup_inputs(seed: int = 0) -> dict:
    seeds = jax.random.split(jax.random.key(seed), 7)
    hidden_in = normal_values(seeds[0], (TOKENS, D), 1.0, 6.0, ((0, 64),))
    request_adapter_keys = jax.random.split(jax.random.fold_in(seeds[1], 1), TOKENS // REQ_DEV)
    request_adapter_turns = jax.random.permutation(jax.random.fold_in(seeds[1], 3), TOKENS // REQ_DEV)
    request_adapter = jax.vmap(lambda own, number: assign_block(jax.random.fold_in(seeds[1], 2), own, number, REQ_DEV, ADAPTERS, 1, MOST, 2))(request_adapter_keys, request_adapter_turns).reshape((TOKENS, 1))
    home_slot = jax.random.permutation(seeds[2], ADAPTERS).astype(jnp.int32)
    gains = jnp.clip(1.0 + 0.1 * jax.random.normal(seeds[3], (N_SEGMENT, D), jnp.float32), 0.5, 1.5)
    shrink_tiles = normal_values(seeds[4], (N_SEGMENT, ADAPTERS, D, RANK), D ** -0.5, 0.0625, ((0, 4), (1, 64)))
    expand_tiles = normal_values(seeds[5], (N_SEGMENT, ADAPTERS, RANK, D), RANK ** -0.5, 0.75, ((0, 4), (1, 64)))
    return dict(hidden_in=hidden_in, request_adapter=request_adapter, home_slot=home_slot, gains=gains, shrink_tiles=shrink_tiles, expand_tiles=expand_tiles)


def normalize(rows, gain):
    values = rows.astype(jnp.float32)
    scale = lax.rsqrt(lax.optimization_barrier(jnp.mean(values * values, axis=-1, keepdims=True)) + 1e-05)
    return (values * scale * gain.astype(jnp.float32)).astype(jnp.bfloat16)

def reference(hidden_in, request_adapter, home_slot, gains, shrink_tiles, expand_tiles):
    adapter_ids = request_adapter[:, 0]
    capacity = MOST * N_ROWS
    current = hidden_in
    outputs = []
    for section in range(N_SEGMENT):
        normed = normalize(current, gains[section])

        def one_adapter(adapter, delta):
            chosen = adapter_ids == adapter
            positions = jnp.nonzero(chosen, size=capacity, fill_value=0)[0]
            valid = (jnp.arange(capacity) < jnp.sum(chosen.astype(jnp.int32)))[:, None]
            storage = home_slot[adapter]
            shrink = lax.dynamic_index_in_dim(shrink_tiles[section], storage, 0, keepdims=False)
            expand = lax.dynamic_index_in_dim(expand_tiles[section], storage, 0, keepdims=False)
            lower = jnp.dot(normed[positions], shrink, preferred_element_type=jnp.float32).astype(jnp.bfloat16)
            term = jnp.dot(lower, expand, preferred_element_type=jnp.float32).astype(jnp.bfloat16)
            term = lax.optimization_barrier(term).astype(jnp.float32)
            return delta.at[positions].add(jnp.where(valid, term, jnp.float32(0.0)))
        delta = lax.fori_loop(0, ADAPTERS, one_adapter, jnp.zeros((TOKENS, D), jnp.float32))
        current = (current.astype(jnp.float32) + delta).astype(jnp.bfloat16)
        outputs.append(current)
    return jnp.stack(outputs)
```

```python
import jax
import jax.numpy as jnp
from jax import lax
from jax.sharding import PartitionSpec as P


def shifted(value, axis, steps):
    count = lax.axis_size(axis)
    return lax.ppermute(value, axis, [(source, (source + steps) % count) for source in range(count)])


def local(hidden_in, request_adapter, home_slot, gains, shrink_tiles, expand_tiles):
    peers = lax.axis_size("rows")
    sections = lax.axis_size("segment")
    plane = lax.axis_index("segment")
    count, width = hidden_in.shape
    part = width // sections
    total = home_slot.shape[0]
    rank = expand_tiles.shape[2]
    depth = max(2, 2 * count // total)
    adapter_ids = request_adapter[:, 0]
    catalog = jnp.arange(total, dtype=jnp.int32)
    storage = jnp.sum(
        jnp.where(adapter_ids[:, None] == catalog[None, :], home_slot[None, :], 0), axis=1
    )
    order = jnp.arange(count, dtype=jnp.int32)
    same_adapter = adapter_ids[:, None] == adapter_ids[None, :]
    earlier = jnp.sum((same_adapter & (order[None, :] < order[:, None])).astype(jnp.int32), axis=1)
    target = storage * depth + earlier
    places = jnp.arange(total * depth, dtype=jnp.int32)
    packing = (places[:, None] == target[None, :]).astype(jnp.bfloat16)
    unpacking = packing.T

    mine = lax.dynamic_slice(hidden_in, (0, plane * part), (count, part))
    packed = jnp.dot(packing, mine, preferred_element_type=jnp.float32).astype(jnp.bfloat16)
    held = lax.all_to_all(
        packed.reshape(peers, depth, part), "rows", split_axis=0, concat_axis=0, tiled=True
    ).reshape(peers * depth, part)

    scaled = (shrink_tiles[0, 0].astype(jnp.float32) * gains[0][:, None]).astype(jnp.bfloat16)
    factors = jnp.concatenate([scaled.T, expand_tiles[0, 0]], axis=0)

    def quarter(steps):
        start = ((plane + steps) % sections) * part
        return lax.dynamic_slice(factors, (0, start), (2 * rank, part))

    arrived = jnp.stack(
        [quarter(0)] + [shifted(quarter(steps), "segment", steps) for steps in range(1, sections)]
    )

    current = held
    results = []
    for section in range(sections):
        own = lax.dynamic_index_in_dim(arrived, (plane - section) % sections, 0, keepdims=False)
        values = current.astype(jnp.float32)
        squares = jnp.sum(values * values, axis=1, keepdims=True)
        product = lax.dot_general(
            current, own[:rank], (((1,), (1,)), ((), ())), preferred_element_type=jnp.float32
        )
        partial = jnp.concatenate([product, jnp.broadcast_to(squares, product.shape)], axis=1)
        summed = partial
        for steps in range(1, sections):
            summed = summed + shifted(partial, "segment", steps)
        scale = lax.rsqrt(summed[:, rank:] / width + 1e-05)
        lower = (summed[:, :rank] * scale).astype(jnp.bfloat16)
        delta = jnp.dot(lower, own[rank:], preferred_element_type=jnp.float32)
        current = (values + delta).astype(jnp.bfloat16)
        results.append(current.reshape(peers, depth, part))

    back = lax.all_to_all(
        jnp.concatenate(results, axis=0),
        ("segment", "rows"),
        split_axis=0,
        concat_axis=0,
        tiled=True,
    ).reshape(sections, total * depth, part)
    rows = [
        jnp.dot(unpacking, back[piece], preferred_element_type=jnp.float32).astype(jnp.bfloat16)
        for piece in range(sections)
    ]
    return jnp.concatenate(rows, axis=1)[None]


def solution(mesh):
    return jax.shard_map(
        local,
        mesh=mesh,
        in_specs=(
            P("rows", None),
            P("rows", None),
            P(),
            P("segment", None),
            P("segment", "rows", None, None),
            P("segment", "rows", None, None),
        ),
        out_specs=P("segment", "rows", None),
        check_vma=False,
    )
```

```python
import jax
import jax.numpy as jnp
from jax import lax
from jax.experimental import pallas as pl
from jax.experimental.pallas import tpu as pltpu
from jax.sharding import PartitionSpec as P

GROUPS = 4
VMEM = pl.BlockSpec(memory_space=pltpu.VMEM)
SMEM = pl.BlockSpec(memory_space=pltpu.SMEM)
F32 = jnp.float32
BF16 = jnp.bfloat16


def shifted(value, axis, steps):
    count = lax.axis_size(axis)
    return lax.ppermute(value, axis, [(source, (source + steps) % count) for source in range(count)])


def dot(a, b, contract_b=0, precision=None):
    return lax.dot_general(
        a, b, (((1,), (contract_b,)), ((), ())), precision=precision, preferred_element_type=F32
    )


def call(kernel, outs, *, scratch=(), flops=0, specs=None, **options):
    return pl.pallas_call(
        kernel,
        out_shape=outs,
        in_specs=specs,
        out_specs=jax.tree.map(lambda _: VMEM, outs),
        scratch_shapes=list(scratch),
        compiler_params=pltpu.CompilerParams(vmem_limit_bytes=48 * 1024 * 1024),
        cost_estimate=pl.CostEstimate(flops=flops, bytes_accessed=4 << 20, transcendentals=0),
        **options,
    )


def pack_kernel(places, hidden, out):
    cols = out.shape[1]
    rows = lax.broadcasted_iota(jnp.int32, (out.shape[0], places.shape[1]), 0)
    chosen = jnp.where(rows == places[...], 1.0, 0.0).astype(BF16)
    stacked = jnp.concatenate(
        [hidden[:, g * cols : (g + 1) * cols] for g in range(GROUPS)], axis=0
    )
    out[...] = dot(chosen, stacked).astype(BF16)


def factors_kernel(depth, order, own, first, second, third, tiles, expand, every):
    rank = expand.shape[0] // 4
    pair = 2 * rank
    for steps, ref in enumerate((own, first, second, third)):
        section = order[steps]
        every[pl.ds(pl.multiple_of(section * pair, pair), pair), :] = ref[...]
    for section in range(4):
        expand[section * rank : (section + 1) * rank] = every[
            section * pair + rank : (section + 1) * pair
        ]
    product = dot(expand[: 3 * rank], every[...], 1)

    def tile(row, section):
        return product[row * rank : (row + 1) * rank, section * pair : (section + 1) * pair]

    lanes = lax.broadcasted_iota(jnp.int32, (rank, pair), 1)

    def last(row):
        return jnp.where(lanes < rank, tile(row, 3), tile(row, row))

    for place, value in enumerate(
        (tile(0, 1), tile(0, 2), tile(1, 2), last(0), last(1), last(2))
    ):
        tiles[place * rank : (place + 1) * rank] = value


def spread(shape, group_axis):
    rows = lax.broadcasted_iota(jnp.int32, shape, group_axis)
    blocks = lax.broadcasted_iota(jnp.int32, shape, 1 - group_axis)
    plain = shape[group_axis] // GROUPS
    group, row = rows // plain, rows % plain
    return jnp.where(blocks == (row // 2) * (2 * GROUPS) + group * 2 + row % 2, 1.0, 0.0).astype(
        BF16
    )


def products_kernel(order, blocks, own, first, second, third, sums, plain):
    count, width = plain.shape
    cols = width // GROUPS
    stacked = dot(spread((blocks.shape[0], blocks.shape[0]), 0), blocks[...]).astype(BF16)
    for g in range(GROUPS):
        plain[:, g * cols : (g + 1) * cols] = stacked[g * count : (g + 1) * count]
    rows = plain[...]
    pair = own.shape[0]
    for steps, ref in enumerate((own, first, second, third)):
        section = order[steps]
        sums[:, pl.ds(pl.multiple_of(section * pair, pair), pair)] = dot(rows, ref[...], 1)
    values = rows.astype(F32)
    squares = jnp.sum(values * values, axis=1, keepdims=True)
    half = pair // 2
    sums[:, 4 * pair - half :] = jnp.broadcast_to(squares, (count, half))


def sections_kernel(
    features, s0, s1, s2, s3, t0, t1, t2, t3, plain, expand, out, stack
):
    rank = expand.shape[0] // 4
    pair = 2 * rank
    count, width = plain.shape
    cols = width // GROUPS
    sums = s0[...] + s1[...] + s2[...] + s3[...]
    tiles = t0[...] + t1[...] + t2[...] + t3[...]
    exact = lax.Precision.HIGHEST

    def tile(place):
        return tiles[place * rank : (place + 1) * rank]

    x01, x02, x12, x03, x13, x23 = (tile(place) for place in range(6))
    y = [sums[:, s * pair : (s + 1) * pair] for s in range(4)]
    square = y[3][:, rank : rank + 1]
    forward = {0: ((1, x01), (2, x02)), 1: ((2, x12),), 2: ()}
    ends = (x03, x13, x23)
    lowers = []
    for s in range(4):
        scale = lax.rsqrt(jnp.maximum(square, 0.0) / features + 1e-05)
        lower = (y[s][:, :rank] * scale).astype(BF16)
        lowers.append(lower)
        if s == 3:
            break
        value = lower.astype(F32)
        for later, x in forward[s]:
            y[later] = y[later] + dot(value, x, 0, exact)
        end = dot(value, ends[s], 0, exact)
        y[3] = y[3] + end
        square = square + jnp.sum(
            value * (2.0 * y[s][:, rank:] + end[:, rank:]), axis=1, keepdims=True
        )
    for g in range(GROUPS):
        columns = slice(g * cols, (g + 1) * cols)
        current = plain[:, columns].astype(F32)
        for s in range(4):
            current = current + dot(lowers[s], expand[s * rank : (s + 1) * rank, columns])
            stack[s, g * count : (g + 1) * count] = current.astype(BF16)
    size = GROUPS * count
    moved = spread((size, size), 1)
    for s in range(4):
        out[s * size : (s + 1) * size] = dot(moved, stack[s]).astype(BF16)


def unpack_kernel(places, back, out):
    size, cols = places.shape[0], back.shape[2]
    count = size // GROUPS
    rows = lax.broadcasted_iota(jnp.int32, (size, back.shape[1]), 1)
    chosen = jnp.where(rows == places[...], 1.0, 0.0).astype(BF16)
    for plane in range(back.shape[0]):
        found = dot(chosen, back[plane]).astype(BF16)
        for g in range(GROUPS):
            start = (plane * GROUPS + g) * cols
            out[:, start : start + cols] = found[g * count : (g + 1) * count]


def local(hidden_in, request_adapter, home_slot, gains, shrink_tiles, expand_tiles):
    peers = lax.axis_size("rows")
    sections = lax.axis_size("segment")
    plane = lax.axis_index("segment")
    count, width = hidden_in.shape
    part = width // sections
    cols = part // GROUPS
    total = home_slot.shape[0]
    rank = expand_tiles.shape[2]
    pair = 2 * rank
    depth = 2
    adapter_ids = request_adapter[:, 0]
    catalog = jnp.arange(total, dtype=jnp.int32)
    storage = jnp.sum(
        jnp.where(adapter_ids[:, None] == catalog[None, :], home_slot[None, :], 0), axis=1
    )
    order = jnp.arange(count, dtype=jnp.int32)
    same_adapter = adapter_ids[:, None] == adapter_ids[None, :]
    earlier = jnp.sum((same_adapter & (order[None, :] < order[:, None])).astype(jnp.int32), axis=1)
    base = storage * (depth * GROUPS) + earlier
    places = (jnp.arange(GROUPS, dtype=jnp.int32)[:, None] * depth + base[None, :]).reshape(-1)
    places_row = places[None, :]
    places_column = places[:, None]
    size = peers * depth * GROUPS

    scaled = (shrink_tiles[0, 0].astype(F32) * gains[0][:, None]).astype(BF16)
    factors = jnp.concatenate([scaled.T, expand_tiles[0, 0]], axis=0)

    def quarter(steps):
        start = ((plane + steps) % sections) * part
        return lax.dynamic_slice(factors, (0, start), (pair, part))

    quarters = [quarter(steps) for steps in range(sections)]
    mine = lax.dynamic_slice(hidden_in, (0, plane * part), (count, part))
    packed = call(
        pack_kernel,
        jax.ShapeDtypeStruct((size, cols), BF16),
        specs=[VMEM, VMEM],
        name="pack",
    )(places_row, mine)
    quarters, packed = lax.optimization_barrier((quarters, packed))
    held = [quarters[0]] + [
        shifted(quarters[steps], "segment", steps) for steps in range(1, sections)
    ]
    arrived = lax.all_to_all(
        packed.reshape(peers, depth * GROUPS, cols), "rows", split_axis=0, concat_axis=0, tiled=True
    ).reshape(size, cols)

    section_order = (plane - jnp.arange(sections, dtype=jnp.int32)) % sections
    tiles, expand = call(
        lambda *refs: factors_kernel(depth, *refs),
        (
            jax.ShapeDtypeStruct((6 * rank, pair), F32),
            jax.ShapeDtypeStruct((sections * rank, part), BF16),
        ),
        scratch=[pltpu.VMEM((sections * pair, part), BF16)],
        specs=[SMEM] + [VMEM] * 4,
        name="factors",
    )(section_order, *held)
    all_tiles = [tiles] + [shifted(tiles, "segment", steps) for steps in range(1, sections)]

    sums, plain = call(
        products_kernel,
        (
            jax.ShapeDtypeStruct((peers * depth, sections * pair), F32),
            jax.ShapeDtypeStruct((peers * depth, part), BF16),
        ),
        specs=[SMEM] + [VMEM] * 5,
        name="products",
    )(section_order, arrived, *held)
    all_sums = [sums] + [shifted(sums, "segment", steps) for steps in range(1, sections)]

    results = call(
        lambda *refs: sections_kernel(width, *refs),
        jax.ShapeDtypeStruct((sections * size, cols), BF16),
        scratch=[pltpu.VMEM((sections, size, cols), BF16)],
        specs=[VMEM] * 10,
        name="sections",
    )(*all_sums, *all_tiles, plain, expand)

    back = lax.all_to_all(
        results.reshape(sections * peers, depth * GROUPS, cols),
        ("segment", "rows"),
        split_axis=0,
        concat_axis=0,
        tiled=True,
    ).reshape(sections, size, cols)
    rows = call(
        unpack_kernel,
        jax.ShapeDtypeStruct((count, width), BF16),
        specs=[VMEM, VMEM],
        name="unpack",
    )(places_column, back)
    return rows[None]


def solution(mesh):
    return jax.shard_map(
        local,
        mesh=mesh,
        in_specs=(
            P("rows", None),
            P("rows", None),
            P(),
            P("segment", None),
            P("segment", "rows", None, None),
            P("segment", "rows", None, None),
        ),
        out_specs=P("segment", "rows", None),
        check_vma=False,
    )
```

```python
import jax
import jax.numpy as jnp
from jax import lax
from jax.experimental import pallas as pl
from jax.experimental.pallas import tpu as pltpu
from jax.sharding import Mesh
from jax.sharding import PartitionSpec as P

GROUPS = 4
VMEM = pl.BlockSpec(memory_space=pltpu.VMEM)
SMEM = pl.BlockSpec(memory_space=pltpu.SMEM)
F32 = jnp.float32
BF16 = jnp.bfloat16


def shifted(value, axis, steps):
    count = lax.axis_size(axis)
    return lax.ppermute(value, axis, [(source, (source + steps) % count) for source in range(count)])


def dot(a, b, contract_b=0, precision=None):
    return lax.dot_general(
        a, b, (((1,), (contract_b,)), ((), ())), precision=precision, preferred_element_type=F32
    )


def call(kernel, outs, *, scratch=(), flops=0, specs=None, **options):
    return pl.pallas_call(
        kernel,
        out_shape=outs,
        in_specs=specs,
        out_specs=jax.tree.map(lambda _: VMEM, outs),
        scratch_shapes=list(scratch),
        compiler_params=pltpu.CompilerParams(vmem_limit_bytes=48 * 1024 * 1024),
        cost_estimate=pl.CostEstimate(flops=flops, bytes_accessed=4 << 20, transcendentals=0),
        **options,
    )


def one_hot(places, shape, axis):
    lines = lax.broadcasted_iota(jnp.int32, shape, axis)
    return jnp.where(lines == places, 1.0, 0.0).astype(BF16)


def block_places(shape, axis, count, core=None, only=None):
    line = lax.broadcasted_iota(jnp.int32, shape, axis)
    group = line // count
    row = line % count
    within = group * 2 + row % 2
    peer = row // 2
    if core is None:
        return peer * (2 * GROUPS) + within
    if only:
        return jnp.where(peer % 2 == core, peer * (2 * GROUPS) + within, -1)
    return jnp.where(peer % 2 == core, -1, (peer // 2) * (2 * GROUPS) + within)


def pack_kernel(places, hidden, out):
    cols = out.shape[1]
    chosen = one_hot(places[...], (out.shape[0], places.shape[1]), 0)
    stacked = jnp.concatenate(
        [hidden[:, g * cols : (g + 1) * cols] for g in range(GROUPS)], axis=0
    )
    out[...] = dot(chosen, stacked).astype(BF16)


def quarters_kernel(plane, shrink, gain, expand, *outs):
    rank = shrink.shape[0]
    part = outs[0].shape[1]
    for steps, out in enumerate(outs):
        start = lax.rem(plane[0] + steps, len(outs)) * part
        columns = pl.ds(pl.multiple_of(start, part), part)
        out[:rank] = (shrink[:, columns].astype(F32) * gain[:, columns]).astype(BF16)
        out[rank:] = expand[:, columns]


def factors_kernel(order, own, first, second, third, tiles, every):
    pair = own.shape[0]
    rank = pair // 2
    for steps, ref in enumerate((own, first, second, third)):
        section = order[steps]
        every[pl.ds(pl.multiple_of(section * pair, pair), pair), :] = ref[...]

    lanes = lax.broadcasted_iota(jnp.int32, (rank, pair), 1)
    needed = every[...]
    place = {(0, 1): 0, (0, 2): 1, (1, 2): 2}
    for row in range(3):
        product = dot(every[row * pair + rank : (row + 1) * pair], needed, 1)

        def tile(section):
            return product[:, section * pair : (section + 1) * pair]

        for section in range(row + 1, 3):
            at = place[row, section] * rank
            tiles[at : at + rank] = tile(section)
        at = (3 + row) * rank
        tiles[at : at + rank] = jnp.where(lanes < rank, tile(3), tile(row))


def products_kernel(order, blocks, others, own, first, second, third, sums, plain):
    count, width = plain.shape
    cols = width // GROUPS
    size = count * GROUPS
    core = order[4]
    stacked = dot(
        one_hot(block_places((size, 1), 0, count, core, True), (size, blocks.shape[0]), 1),
        blocks[...],
    ) + dot(
        one_hot(block_places((size, 1), 0, count, core, False), (size, others.shape[0]), 1),
        others[...],
    )
    stacked = stacked.astype(BF16)
    for g in range(GROUPS):
        plain[:, g * cols : (g + 1) * cols] = stacked[g * count : (g + 1) * count]
    rows = plain[...]
    pair = own.shape[0]
    for steps, ref in enumerate((own, first, second, third)):
        section = order[steps]
        sums[:, pl.ds(pl.multiple_of(section * pair, pair), pair)] = dot(rows, ref[...], 1)
    values = rows.astype(F32)
    squares = jnp.sum(values * values, axis=1, keepdims=True)
    half = pair // 2
    sums[:, 4 * pair - half :] = jnp.broadcast_to(squares, (count, half))


def sections_kernel(
    features, order, s0, s1, s2, s3, t0, t1, t2, t3, plain, f0, f1, f2, f3, out, stack, expand
):
    pair = f0.shape[0]
    rank = pair // 2
    count, width = plain.shape
    cols = width // GROUPS
    for steps, ref in enumerate((f0, f1, f2, f3)):
        section = order[steps]
        expand[pl.ds(pl.multiple_of(section * rank, rank), rank), :] = ref[rank:]
    sums = s0[...] + s1[...] + s2[...] + s3[...]
    tiles = t0[...] + t1[...] + t2[...] + t3[...]
    exact = lax.Precision.HIGHEST

    def tile(place):
        return tiles[place * rank : (place + 1) * rank]

    x01, x02, x12, x03, x13, x23 = (tile(place) for place in range(6))
    y = [sums[:, s * pair : (s + 1) * pair] for s in range(4)]
    square = y[3][:, rank : rank + 1]
    forward = {0: ((1, x01), (2, x02)), 1: ((2, x12),), 2: ()}
    ends = (x03, x13, x23)
    lowers = []
    for s in range(4):
        scale = lax.rsqrt(jnp.maximum(square, 0.0) / features + 1e-05)
        lower = (y[s][:, :rank] * scale).astype(BF16)
        lowers.append(lower)
        if s == 3:
            break
        value = lower.astype(F32)
        for later, x in forward[s]:
            y[later] = y[later] + dot(value, x, 0, exact)
        end = dot(value, ends[s], 0, exact)
        y[3] = y[3] + end
        square = square + jnp.sum(
            value * (2.0 * y[s][:, rank:] + end[:, rank:]), axis=1, keepdims=True
        )
    for g in range(GROUPS):
        columns = slice(g * cols, (g + 1) * cols)
        current = plain[:, columns].astype(F32)
        for s in range(4):
            current = current + dot(lowers[s], expand[s * rank : (s + 1) * rank, columns])
            stack[s, g * count : (g + 1) * count] = current.astype(BF16)
    size = GROUPS * count
    moved = one_hot(block_places((1, size), 1, count), (size, size), 0)
    for s in range(4):
        out[s * size : (s + 1) * size] = dot(moved, stack[s]).astype(BF16)


def place_rows(out, found, count, cols, plane):
    for g in range(GROUPS):
        start = (plane * GROUPS + g) * cols
        out[:, start : start + cols] = found[g * count : (g + 1) * count]


def unpack_kernel(places, back, out):
    size, cols = places.shape[0], back.shape[2]
    chosen = one_hot(places[...], (size, back.shape[1]), 1)
    for plane in range(back.shape[0]):
        found = dot(chosen, back[plane]).astype(BF16)
        place_rows(out, found, size // GROUPS, cols, plane)


def finish_kernel(places, back, begun, out):
    size, cols = places.shape[0], back.shape[2]
    count = size // GROUPS
    chosen = one_hot(places[...], (size, back.shape[1]), 1)
    for plane in range(back.shape[0]):
        found = dot(chosen, back[plane])
        for g in range(GROUPS):
            start = (plane * GROUPS + g) * cols
            kept = begun[:, start : start + cols].astype(F32)
            out[:, start : start + cols] = (kept + found[g * count : (g + 1) * count]).astype(BF16)


def local(hidden_in, request_adapter, home_slot, gains, shrink_tiles, expand_tiles):
    chips = lax.axis_size("chip")
    peers = 2 * chips
    sections = lax.axis_size("segment")
    plane = lax.axis_index("segment")
    core = lax.axis_index("core")
    count, width = hidden_in.shape
    part = width // sections
    cols = part // GROUPS
    total = home_slot.shape[0]
    rank = expand_tiles.shape[2]
    pair = 2 * rank
    depth = 2
    block = depth * GROUPS
    size = peers * block

    quarters = call(
        quarters_kernel,
        tuple(jax.ShapeDtypeStruct((pair, part), BF16) for _ in range(sections)),
        specs=[SMEM, VMEM, VMEM, VMEM],
        name="quarters",
    )(plane.reshape(1), shrink_tiles[0, 0].T, gains, expand_tiles[0, 0])

    adapter_ids = request_adapter[:, 0]
    catalog = jnp.arange(total, dtype=jnp.int32)
    storage = jnp.sum(
        jnp.where(adapter_ids[:, None] == catalog[None, :], home_slot[None, :], 0), axis=1
    )
    order = jnp.arange(count, dtype=jnp.int32)
    same_adapter = adapter_ids[:, None] == adapter_ids[None, :]
    earlier = jnp.sum((same_adapter & (order[None, :] < order[:, None])).astype(jnp.int32), axis=1)
    groups = jnp.arange(GROUPS, dtype=jnp.int32)[:, None] * depth

    def grouped(base):
        return jnp.where(base[None, :] < 0, -1, groups + base[None, :]).reshape(-1)

    near = storage % 2 == core
    homes = grouped(storage * block + earlier)[None, :]
    near_places = grouped(
        jnp.where(near, (storage // 2) * (2 * block) + core * block + earlier, -1)
    )[:, None]
    far_places = grouped(jnp.where(near, -1, (storage // 2) * block + earlier))[:, None]

    mine = lax.dynamic_slice(hidden_in, (0, plane * part), (count, part))
    packed = call(
        pack_kernel,
        jax.ShapeDtypeStruct((size, cols), BF16),
        specs=[VMEM, VMEM],
        name="pack",
    )(homes, mine)
    held = [quarters[0]] + [
        shifted(quarters[steps], "segment", steps) for steps in range(1, sections)
    ]

    def other_core(blocks):
        lead = blocks.shape[0]
        theirs = lax.dynamic_slice(blocks, (0, (1 - core) * block, 0), (lead, block, cols))
        return lax.ppermute(theirs, "core", [(0, 1), (1, 0)])

    arrived = lax.all_to_all(
        packed.reshape(chips, 2 * block, cols), "chip", split_axis=0, concat_axis=0, tiled=True
    )
    others = other_core(arrived).reshape(chips * block, cols)

    section_order = (plane - jnp.arange(sections, dtype=jnp.int32)) % sections
    section_order = jnp.concatenate([section_order, core.reshape(1)])
    tiles = call(
        factors_kernel,
        jax.ShapeDtypeStruct((6 * rank, pair), F32),
        scratch=[pltpu.VMEM((sections * pair, part), BF16)],
        specs=[SMEM] + [VMEM] * 4,
        name="factors",
    )(section_order, *held)
    all_tiles = [tiles] + [shifted(tiles, "segment", steps) for steps in range(1, sections)]

    sums, plain = call(
        products_kernel,
        (
            jax.ShapeDtypeStruct((peers * depth, sections * pair), F32),
            jax.ShapeDtypeStruct((peers * depth, part), BF16),
        ),
        specs=[SMEM] + [VMEM] * 6,
        name="products",
    )(section_order, arrived.reshape(size, cols), others, *held)
    all_sums = [sums] + [shifted(sums, "segment", steps) for steps in range(1, sections)]

    results = call(
        lambda *refs: sections_kernel(width, *refs),
        jax.ShapeDtypeStruct((sections * size, cols), BF16),
        scratch=[
            pltpu.VMEM((sections, size, cols), BF16),
            pltpu.VMEM((sections * rank, part), BF16),
        ],
        specs=[SMEM] + [VMEM] * 13,
        name="sections",
    )(section_order, *all_sums, *all_tiles, plain, *held)

    back = lax.all_to_all(
        results.reshape(sections * chips, 2 * block, cols),
        ("segment", "chip"),
        split_axis=0,
        concat_axis=0,
        tiled=True,
    )
    others = other_core(back).reshape(sections, chips * block, cols)
    begun = call(
        unpack_kernel,
        jax.ShapeDtypeStruct((count, width), BF16),
        specs=[VMEM, VMEM],
        name="unpack",
    )(near_places, back.reshape(sections, size, cols))
    rows = call(
        finish_kernel,
        jax.ShapeDtypeStruct((count, width), BF16),
        specs=[VMEM, VMEM, VMEM],
        name="finish",
    )(far_places, others, begun)
    return rows[None]


def solution(mesh):
    planes, peers = mesh.devices.shape
    split = Mesh(mesh.devices.reshape(planes, peers // 2, 2), ("segment", "chip", "core"))
    rows = ("chip", "core")
    return jax.shard_map(
        local,
        mesh=split,
        in_specs=(
            P(rows, None),
            P(rows, None),
            P(),
            P("segment", None),
            P("segment", rows, None, None),
            P("segment", rows, None, None),
        ),
        out_specs=P("segment", rows, None),
        check_vma=False,
    )
```

```python
import jax
import jax.numpy as jnp
from jax import lax
from jax.experimental import pallas as pl
from jax.experimental.pallas import tpu as pltpu
from jax.sharding import Mesh
from jax.sharding import PartitionSpec as P

GROUPS = 4
FACTOR_FLOPS = 40_000_000_000
VMEM = pl.BlockSpec(memory_space=pltpu.VMEM)
SMEM = pl.BlockSpec(memory_space=pltpu.SMEM)
F32 = jnp.float32
BF16 = jnp.bfloat16


def shifted(value, axis, steps):
    count = lax.axis_size(axis)
    return lax.ppermute(value, axis, [(source, (source + steps) % count) for source in range(count)])


def dot(a, b, contract_b=0, precision=None):
    return lax.dot_general(
        a, b, (((1,), (contract_b,)), ((), ())), precision=precision, preferred_element_type=F32
    )


def call(kernel, outs, *, scratch=(), flops=0, specs=None, **options):
    return pl.pallas_call(
        kernel,
        out_shape=outs,
        in_specs=specs,
        out_specs=jax.tree.map(lambda _: VMEM, outs),
        scratch_shapes=list(scratch),
        compiler_params=pltpu.CompilerParams(vmem_limit_bytes=48 * 1024 * 1024),
        cost_estimate=pl.CostEstimate(flops=flops, bytes_accessed=4 << 20, transcendentals=0),
        **options,
    )


def one_hot(places, shape, axis):
    lines = lax.broadcasted_iota(jnp.int32, shape, axis)
    return jnp.where(lines == places, 1.0, 0.0).astype(BF16)


def block_places(shape, axis, count, core=None, only=None):
    line = lax.broadcasted_iota(jnp.int32, shape, axis)
    group = line // count
    row = line % count
    within = group * 2 + row % 2
    peer = row // 2
    if core is None:
        return peer * (2 * GROUPS) + within
    if only:
        return jnp.where(peer % 2 == core, peer * (2 * GROUPS) + within, -1)
    return jnp.where(peer % 2 == core, -1, (peer // 2) * (2 * GROUPS) + within)


def pack_kernel(places, hidden, out):
    cols = out.shape[1]
    chosen = one_hot(places[...], (out.shape[0], places.shape[1]), 0)
    stacked = jnp.concatenate(
        [hidden[:, g * cols : (g + 1) * cols] for g in range(GROUPS)], axis=0
    )
    out[...] = dot(chosen, stacked).astype(BF16)


def quarters_kernel(plane, shrink, gain, expand, *outs):
    rank = shrink.shape[0]
    part = outs[0].shape[1]
    for steps, out in enumerate(outs):
        start = lax.rem(plane[0] + steps, len(outs)) * part
        columns = pl.ds(pl.multiple_of(start, part), part)
        out[:rank] = (shrink[:, columns].astype(F32) * gain[:, columns]).astype(BF16)
        out[rank:] = expand[:, columns]


def factors_kernel(order, own, first, second, third, tiles, every, expand):
    pair = own.shape[0]
    rank = pair // 2
    for steps, ref in enumerate((own, first, second, third)):
        section = order[steps]
        every[pl.ds(pl.multiple_of(section * pair, pair), pair), :] = ref[...]
        expand[pl.ds(pl.multiple_of(section * rank, rank), rank), :] = ref[rank:]
    product = dot(expand[: 3 * rank], every[...], 1)

    def tile(row, section):
        return product[row * rank : (row + 1) * rank, section * pair : (section + 1) * pair]

    lanes = lax.broadcasted_iota(jnp.int32, (rank, pair), 1)

    def last(row):
        return jnp.where(lanes < rank, tile(row, 3), tile(row, row))

    for place, value in enumerate(
        (tile(0, 1), tile(0, 2), tile(1, 2), last(0), last(1), last(2))
    ):
        tiles[place * rank : (place + 1) * rank] = value


def products_kernel(order, blocks, others, own, first, second, third, sums, plain):
    count, width = plain.shape
    cols = width // GROUPS
    size = count * GROUPS
    core = order[4]
    stacked = dot(
        one_hot(block_places((size, 1), 0, count, core, True), (size, blocks.shape[0]), 1),
        blocks[...],
    ) + dot(
        one_hot(block_places((size, 1), 0, count, core, False), (size, others.shape[0]), 1),
        others[...],
    )
    stacked = stacked.astype(BF16)
    for g in range(GROUPS):
        plain[:, g * cols : (g + 1) * cols] = stacked[g * count : (g + 1) * count]
    rows = plain[...]
    pair = own.shape[0]
    for steps, ref in enumerate((own, first, second, third)):
        section = order[steps]
        sums[:, pl.ds(pl.multiple_of(section * pair, pair), pair)] = dot(rows, ref[...], 1)
    values = rows.astype(F32)
    squares = jnp.sum(values * values, axis=1, keepdims=True)
    half = pair // 2
    sums[:, 4 * pair - half :] = jnp.broadcast_to(squares, (count, half))


def sections_kernel(
    features, order, s0, s1, s2, s3, t0, t1, t2, t3, plain, f0, f1, f2, f3, out, stack, expand
):
    pair = f0.shape[0]
    rank = pair // 2
    count, width = plain.shape
    cols = width // GROUPS
    for steps, ref in enumerate((f0, f1, f2, f3)):
        section = order[steps]
        expand[pl.ds(pl.multiple_of(section * rank, rank), rank), :] = ref[rank:]
    sums = s0[...] + s1[...] + s2[...] + s3[...]
    tiles = t0[...] + t1[...] + t2[...] + t3[...]
    exact = lax.Precision.HIGHEST

    def tile(place):
        return tiles[place * rank : (place + 1) * rank]

    x01, x02, x12, x03, x13, x23 = (tile(place) for place in range(6))
    y = [sums[:, s * pair : (s + 1) * pair] for s in range(4)]
    square = y[3][:, rank : rank + 1]
    forward = {0: ((1, x01), (2, x02)), 1: ((2, x12),), 2: ()}
    ends = (x03, x13, x23)
    lowers = []
    for s in range(4):
        scale = lax.rsqrt(jnp.maximum(square, 0.0) / features + 1e-05)
        lower = (y[s][:, :rank] * scale).astype(BF16)
        lowers.append(lower)
        if s == 3:
            break
        value = lower.astype(F32)
        for later, x in forward[s]:
            y[later] = y[later] + dot(value, x, 0, exact)
        end = dot(value, ends[s], 0, exact)
        y[3] = y[3] + end
        square = square + jnp.sum(
            value * (2.0 * y[s][:, rank:] + end[:, rank:]), axis=1, keepdims=True
        )
    for g in range(GROUPS):
        columns = slice(g * cols, (g + 1) * cols)
        current = plain[:, columns].astype(F32)
        for s in range(4):
            current = current + dot(lowers[s], expand[s * rank : (s + 1) * rank, columns])
            stack[s, g * count : (g + 1) * count] = current.astype(BF16)
    size = GROUPS * count
    moved = one_hot(block_places((1, size), 1, count), (size, size), 0)
    for s in range(4):
        out[s * size : (s + 1) * size] = dot(moved, stack[s]).astype(BF16)


def unpack_kernel(places, back, out):
    size, cols = places.shape[0], back.shape[2]
    count = size // GROUPS
    chosen = one_hot(places[...], (size, back.shape[1]), 1)
    for plane in range(back.shape[0]):
        found = dot(chosen, back[plane]).astype(BF16)
        for g in range(GROUPS):
            start = (plane * GROUPS + g) * cols
            out[:, start : start + cols] = found[g * count : (g + 1) * count]


def local(hidden_in, request_adapter, home_slot, gains, shrink_tiles, expand_tiles):
    chips = lax.axis_size("chip")
    peers = 2 * chips
    sections = lax.axis_size("segment")
    plane = lax.axis_index("segment")
    core = lax.axis_index("core")
    count, width = hidden_in.shape
    part = width // sections
    cols = part // GROUPS
    total = home_slot.shape[0]
    rank = expand_tiles.shape[2]
    pair = 2 * rank
    depth = 2
    block = depth * GROUPS
    size = peers * block

    quarters = call(
        quarters_kernel,
        tuple(jax.ShapeDtypeStruct((pair, part), BF16) for _ in range(sections)),
        specs=[SMEM, VMEM, VMEM, VMEM],
        name="quarters",
    )(plane.reshape(1), shrink_tiles[0, 0].T, gains, expand_tiles[0, 0])

    adapter_ids = request_adapter[:, 0]
    catalog = jnp.arange(total, dtype=jnp.int32)
    storage = jnp.sum(
        jnp.where(adapter_ids[:, None] == catalog[None, :], home_slot[None, :], 0), axis=1
    )
    order = jnp.arange(count, dtype=jnp.int32)
    same_adapter = adapter_ids[:, None] == adapter_ids[None, :]
    earlier = jnp.sum((same_adapter & (order[None, :] < order[:, None])).astype(jnp.int32), axis=1)
    groups = jnp.arange(GROUPS, dtype=jnp.int32)[:, None] * depth
    homes = (groups + (storage * block + earlier)[None, :]).reshape(-1)

    mine = lax.dynamic_slice(hidden_in, (0, plane * part), (count, part))
    packed = call(
        pack_kernel,
        jax.ShapeDtypeStruct((size, cols), BF16),
        specs=[VMEM, VMEM],
        name="pack",
    )(homes[None, :], mine)
    held = [quarters[0]] + [
        shifted(quarters[steps], "segment", steps) for steps in range(1, sections)
    ]

    arrived = lax.all_to_all(
        packed.reshape(chips, 2 * block, cols), "chip", split_axis=0, concat_axis=0, tiled=True
    )

    section_order = (plane - jnp.arange(sections, dtype=jnp.int32)) % sections
    section_order = jnp.concatenate([section_order, core.reshape(1)])
    tiles = call(
        factors_kernel,
        jax.ShapeDtypeStruct((6 * rank, pair), F32),
        scratch=[
            pltpu.VMEM((sections * pair, part), BF16),
            pltpu.VMEM((sections * rank, part), BF16),
        ],
        specs=[SMEM] + [VMEM] * 4,
        flops=FACTOR_FLOPS,
        name="factors",
    )(section_order, *held)
    arrived, tiles = lax.optimization_barrier((arrived, tiles))
    all_tiles = [tiles] + [shifted(tiles, "segment", steps) for steps in range(1, sections)]

    theirs = lax.dynamic_slice(arrived, (0, (1 - core) * block, 0), (chips, block, cols))
    others = lax.ppermute(theirs, "core", [(0, 1), (1, 0)]).reshape(chips * block, cols)
    sums, plain = call(
        products_kernel,
        (
            jax.ShapeDtypeStruct((peers * depth, sections * pair), F32),
            jax.ShapeDtypeStruct((peers * depth, part), BF16),
        ),
        specs=[SMEM] + [VMEM] * 6,
        name="products",
    )(section_order, arrived.reshape(size, cols), others, *held)
    all_sums = [sums] + [shifted(sums, "segment", steps) for steps in range(1, sections)]

    results = call(
        lambda *refs: sections_kernel(width, *refs),
        jax.ShapeDtypeStruct((sections * size, cols), BF16),
        scratch=[
            pltpu.VMEM((sections, size, cols), BF16),
            pltpu.VMEM((sections * rank, part), BF16),
        ],
        specs=[SMEM] + [VMEM] * 13,
        name="sections",
    )(section_order, *all_sums, *all_tiles, plain, *held)

    back = lax.all_to_all(
        results.reshape(sections * peers, block, cols),
        ("segment", "chip", "core"),
        split_axis=0,
        concat_axis=0,
        tiled=True,
    )
    rows = call(
        unpack_kernel,
        jax.ShapeDtypeStruct((count, width), BF16),
        specs=[VMEM, VMEM],
        name="unpack",
    )(homes[:, None], back.reshape(sections, size, cols))
    return rows[None]


def solution(mesh):
    planes, peers = mesh.devices.shape
    split = Mesh(mesh.devices.reshape(planes, peers // 2, 2), ("segment", "chip", "core"))
    rows = ("chip", "core")
    return jax.shard_map(
        local,
        mesh=split,
        in_specs=(
            P(rows, None),
            P(rows, None),
            P(),
            P("segment", None),
            P("segment", rows, None, None),
            P("segment", rows, None, None),
        ),
        out_specs=P("segment", rows, None),
        check_vma=False,
    )
```

```python
import jax
import jax.numpy as jnp
from jax import lax
from jax.experimental import pallas as pl
from jax.experimental.pallas import tpu as pltpu
from jax.sharding import Mesh
from jax.sharding import PartitionSpec as P

GROUPS = 4
FACTOR_FLOPS = 40_000_000_000
VMEM = pl.BlockSpec(memory_space=pltpu.VMEM)
ANY = pl.BlockSpec(memory_space=pl.ANY)
SMEM = pl.BlockSpec(memory_space=pltpu.SMEM)
F32 = jnp.float32
BF16 = jnp.bfloat16


def shifted(value, axis, steps):
    count = lax.axis_size(axis)
    return lax.ppermute(value, axis, [(source, (source + steps) % count) for source in range(count)])


def dot(a, b, contract_b=0, precision=None):
    return lax.dot_general(
        a, b, (((1,), (contract_b,)), ((), ())), precision=precision, preferred_element_type=F32
    )


def call(kernel, outs, *, scratch=(), flops=0, specs=None, out_spec=VMEM, room=48, **options):
    return pl.pallas_call(
        kernel,
        out_shape=outs,
        in_specs=specs,
        out_specs=jax.tree.map(lambda _: out_spec, outs),
        scratch_shapes=list(scratch),
        compiler_params=pltpu.CompilerParams(vmem_limit_bytes=room * 1024 * 1024),
        cost_estimate=pl.CostEstimate(flops=flops, bytes_accessed=4 << 20, transcendentals=0),
        **options,
    )


def one_hot(places, shape, axis):
    lines = lax.broadcasted_iota(jnp.int32, shape, axis)
    return jnp.where(lines == places, 1.0, 0.0).astype(BF16)


def block_places(shape, axis, count, core=None, only=None):
    line = lax.broadcasted_iota(jnp.int32, shape, axis)
    group = line // count
    row = line % count
    within = group * 2 + row % 2
    peer = row // 2
    if core is None:
        return peer * (2 * GROUPS) + within
    if only:
        return jnp.where(peer % 2 == core, peer * (2 * GROUPS) + within, -1)
    return jnp.where(peer % 2 == core, -1, (peer // 2) * (2 * GROUPS) + within)


def quarter_columns(plane, steps, part, planes=4):
    return pl.ds(pl.multiple_of(lax.rem(plane + steps, planes) * part, part), part)


def pack_kernel(plane, places, hidden, out, mine, arrival):
    cols = out.shape[1]
    part = mine.shape[1]
    copy = pltpu.make_async_copy(
        hidden.at[:, quarter_columns(plane[0], 0, part)], mine, arrival
    )
    copy.start()
    chosen = one_hot(places[...], (out.shape[0], places.shape[1]), 0)
    copy.wait()
    stacked = jnp.concatenate([mine[:, g * cols : (g + 1) * cols] for g in range(GROUPS)], axis=0)
    out[...] = dot(chosen, stacked).astype(BF16)


def quarters_kernel(
    plane, shrink, gain, expand, q0, q1, q2, q3, taken, weights, made, gain_in, in_sem, put_sem, out_sem
):
    rank = shrink.shape[0]
    outs = (q0, q1, q2, q3)
    part = q0.shape[1]
    columns = [quarter_columns(plane[0], steps, part) for steps in range(4)]
    order = (2, 1, 3, 0)
    load = pltpu.make_async_copy(gain, weights, gain_in)
    load.start()
    ins, puts, sends = {}, {}, {}
    for k in order:
        ins[k] = pltpu.make_async_copy(shrink.at[:, columns[k]], taken.at[k], in_sem.at[k])
        ins[k].start()
    for k in order:
        puts[k] = pltpu.make_async_copy(
            expand.at[:, columns[k]], outs[k].at[pl.ds(rank, rank)], put_sem.at[k]
        )
        puts[k].start()
    load.wait()
    for k in order:
        ins[k].wait()
        made[k] = (taken[k].astype(F32) * weights[:, columns[k]]).astype(BF16)
        sends[k] = pltpu.make_async_copy(made.at[k], outs[k].at[pl.ds(0, rank)], out_sem.at[k])
        sends[k].start()
    for k in order:
        puts[k].wait()
        sends[k].wait()


def factors_kernel(order, own, first, second, third, tiles, every, expand):
    pair = own.shape[0]
    rank = pair // 2
    for steps, ref in enumerate((own, first, second, third)):
        section = order[steps]
        every[pl.ds(pl.multiple_of(section * pair, pair), pair), :] = ref[...]
        expand[pl.ds(pl.multiple_of(section * rank, rank), rank), :] = ref[rank:]
    product = dot(expand[: 3 * rank], every[...], 1)

    def tile(row, section):
        return product[row * rank : (row + 1) * rank, section * pair : (section + 1) * pair]

    lanes = lax.broadcasted_iota(jnp.int32, (rank, pair), 1)

    def last(row):
        return jnp.where(lanes < rank, tile(row, 3), tile(row, row))

    for place, value in enumerate(
        (tile(0, 1), tile(0, 2), tile(1, 2), last(0), last(1), last(2))
    ):
        tiles[place * rank : (place + 1) * rank] = value


def rounded(value):
    high = value.astype(BF16)
    return high, value - high.astype(F32)


def products_kernel(
    order, blocks, others, tiles, own, first, second, third, sums, plain, product
):
    count, width = plain.shape
    cols = width // GROUPS
    size = count * GROUPS
    core = order[4]
    stacked = dot(
        one_hot(block_places((size, 1), 0, count, core, True), (size, blocks.shape[0]), 1),
        blocks[...],
    ) + dot(
        one_hot(block_places((size, 1), 0, count, core, False), (size, others.shape[0]), 1),
        others[...],
    )
    stacked = stacked.astype(BF16)
    for g in range(GROUPS):
        plain[:, g * cols : (g + 1) * cols] = stacked[g * count : (g + 1) * count]
    rows = plain[...]
    pair = own.shape[0]
    half = pair // 2
    for steps, ref in enumerate((own, first, second, third)):
        section = order[steps]
        product[:, pl.ds(pl.multiple_of(section * pair, pair), pair)] = dot(rows, ref[...], 1)
    values = rows.astype(F32)
    squares = jnp.sum(values * values, axis=1, keepdims=True)
    lanes = lax.broadcasted_iota(jnp.int32, (count, pair), 1)
    low = []
    for s in range(3):
        high, rest = rounded(product[:, s * pair : (s + 1) * pair])
        sums[:, s * pair : (s + 1) * pair] = high
        low.append(rest)
    high, rest = rounded(squares)
    ends = jnp.where(lanes < half, product[:, 3 * pair :], high.astype(F32))
    sums[:, 3 * pair : 4 * pair] = jnp.where(lanes < half + half // 2, ends, rest).astype(BF16)
    tile_low = []
    for at in range(3):
        high, rest = rounded(tiles[at * pair : (at + 1) * pair])
        sums[:, (6 + at) * pair : (7 + at) * pair] = high
        tile_low.append(rest)

    def both(left, right):
        return jnp.where(lanes < half, pltpu.roll(left, half, 1), right).astype(BF16)

    sums[:, 4 * pair : 5 * pair] = both(low[1], low[0])
    sums[:, 5 * pair : 6 * pair] = both(tile_low[2], low[2])
    sums[:, 9 * pair :] = both(tile_low[1], tile_low[0])


def sections_kernel(
    features, order, s0, s1, s2, s3, plain, f0, f1, f2, f3, out, stack, expand
):
    pair = f0.shape[0]
    rank = pair // 2
    count, width = plain.shape
    cols = width // GROUPS
    for steps, ref in enumerate((f0, f1, f2, f3)):
        section = order[steps]
        expand[pl.ds(pl.multiple_of(section * rank, rank), rank), :] = ref[rank:]
    lanes = lax.broadcasted_iota(jnp.int32, (count, pair), 1)

    def summed(at):
        columns = slice(at * pair, (at + 1) * pair)
        parts = [ref[:, columns].astype(F32) for ref in (s0, s1, s2, s3)]
        return (parts[0] + parts[1]) + (parts[2] + parts[3])

    def right(value):
        return jnp.where(lanes < rank, 0.0, value)

    def left(value):
        return right(pltpu.roll(value, rank, 1))

    low, mixed, tile_low = summed(4), summed(5), summed(9)
    y = [summed(0) + right(low), summed(1) + left(low), summed(2) + right(mixed), summed(3)]
    square = y[3][:, rank : rank + 1] + y[3][:, pair - 1 :]
    stacks = [summed(6) + right(tile_low), summed(7) + left(tile_low), summed(8) + left(mixed)]

    def thirds(place):
        at = (place % 2) * rank
        value = stacks[place // 2][at : at + rank]
        high, rest = rounded(value)
        middle, rest = rounded(rest)
        return jnp.concatenate([high, middle, rest.astype(BF16)], axis=0)

    uses = (((1, 0), (2, 1), (3, 3)), ((2, 2), (3, 4)), ((3, 5),))
    lowers = []
    for s in range(4):
        scale = lax.rsqrt(jnp.maximum(square, 0.0) / features + 1e-05)
        lower = (y[s][:, :rank] * scale).astype(BF16)
        lowers.append(lower)
        if s == 3:
            break
        added = dot(
            jnp.concatenate([lower] * 3, axis=1),
            jnp.concatenate([thirds(place) for _, place in uses[s]], axis=1),
        )
        value = lower.astype(F32)
        for at, (later, _) in enumerate(uses[s]):
            y[later] = y[later] + added[:, at * pair : (at + 1) * pair]
        ends = added[:, added.shape[1] - rank :]
        square = square + jnp.sum(value * (2.0 * y[s][:, rank:] + ends), axis=1, keepdims=True)
    for g in range(GROUPS):
        columns = slice(g * cols, (g + 1) * cols)
        current = plain[:, columns].astype(F32)
        for s in range(4):
            current = current + dot(lowers[s], expand[s * rank : (s + 1) * rank, columns])
            stack[s, g * count : (g + 1) * count] = current.astype(BF16)
    size = GROUPS * count
    moved = one_hot(block_places((1, size), 1, count), (size, size), 0)
    for s in range(4):
        out[s * size : (s + 1) * size] = dot(moved, stack[s]).astype(BF16)


def unpack_kernel(places, back, out):
    size, cols = places.shape[0], back.shape[2]
    count = size // GROUPS
    chosen = one_hot(places[...], (size, back.shape[1]), 1)
    for plane in range(back.shape[0]):
        found = dot(chosen, back[plane]).astype(BF16)
        for g in range(GROUPS):
            start = (plane * GROUPS + g) * cols
            out[:, start : start + cols] = found[g * count : (g + 1) * count]


def local(hidden_in, request_adapter, home_slot, gains, shrink_tiles, expand_tiles):
    chips = lax.axis_size("chip")
    peers = 2 * chips
    sections = lax.axis_size("segment")
    plane = lax.axis_index("segment")
    core = lax.axis_index("core")
    count, width = hidden_in.shape
    part = width // sections
    cols = part // GROUPS
    total = home_slot.shape[0]
    rank = expand_tiles.shape[2]
    pair = 2 * rank
    depth = 2
    block = depth * GROUPS
    size = peers * block

    quarters = call(
        quarters_kernel,
        tuple(jax.ShapeDtypeStruct((pair, part), BF16) for _ in range(sections)),
        scratch=[
            pltpu.VMEM((sections, rank, part), BF16),
            pltpu.VMEM((1, width), F32),
            pltpu.VMEM((sections, rank, part), BF16),
            pltpu.SemaphoreType.DMA,
            pltpu.SemaphoreType.DMA((sections,)),
            pltpu.SemaphoreType.DMA((sections,)),
            pltpu.SemaphoreType.DMA((sections,)),
        ],
        specs=[SMEM, ANY, ANY, ANY],
        out_spec=ANY,
        room=60,
        name="quarters",
    )(plane.reshape(1), shrink_tiles[0, 0].T, gains, expand_tiles[0, 0])

    adapter_ids = request_adapter[:, 0]
    catalog = jnp.arange(total, dtype=jnp.int32)
    storage = jnp.sum(
        jnp.where(adapter_ids[:, None] == catalog[None, :], home_slot[None, :], 0), axis=1
    )
    order = jnp.arange(count, dtype=jnp.int32)
    same_adapter = adapter_ids[:, None] == adapter_ids[None, :]
    earlier = jnp.sum((same_adapter & (order[None, :] < order[:, None])).astype(jnp.int32), axis=1)
    groups = jnp.arange(GROUPS, dtype=jnp.int32)[:, None] * depth
    homes = (groups + (storage * block + earlier)[None, :]).reshape(-1)

    packed = call(
        pack_kernel,
        jax.ShapeDtypeStruct((size, cols), BF16),
        scratch=[pltpu.VMEM((count, part), BF16), pltpu.SemaphoreType.DMA],
        specs=[SMEM, VMEM, ANY],
        room=60,
        name="pack",
    )(plane.reshape(1), homes[None, :], hidden_in)
    held = [quarters[0]] + [
        shifted(quarters[steps], "segment", steps) for steps in range(1, sections)
    ]

    arrived = lax.all_to_all(
        packed.reshape(chips, 2 * block, cols), "chip", split_axis=0, concat_axis=0, tiled=True
    )

    section_order = (plane - jnp.arange(sections, dtype=jnp.int32)) % sections
    section_order = jnp.concatenate([section_order, core.reshape(1)])
    tiles = call(
        factors_kernel,
        jax.ShapeDtypeStruct((6 * rank, pair), F32),
        scratch=[
            pltpu.VMEM((sections * pair, part), BF16),
            pltpu.VMEM((sections * rank, part), BF16),
        ],
        specs=[SMEM] + [VMEM] * 4,
        flops=FACTOR_FLOPS,
        name="factors",
    )(section_order, *held)
    arrived, tiles = lax.optimization_barrier((arrived, tiles))

    theirs = lax.dynamic_slice(arrived, (0, (1 - core) * block, 0), (chips, block, cols))
    others = lax.ppermute(theirs, "core", [(0, 1), (1, 0)]).reshape(chips * block, cols)
    sums, plain = call(
        products_kernel,
        (
            jax.ShapeDtypeStruct((peers * depth, 10 * pair), BF16),
            jax.ShapeDtypeStruct((peers * depth, part), BF16),
        ),
        scratch=[pltpu.VMEM((peers * depth, sections * pair), F32)],
        specs=[SMEM] + [VMEM] * 7,
        name="products",
    )(section_order, arrived.reshape(size, cols), others, tiles, *held)
    all_sums = [sums] + [shifted(sums, "segment", steps) for steps in range(1, sections)]

    results = call(
        lambda *refs: sections_kernel(width, *refs),
        jax.ShapeDtypeStruct((sections * size, cols), BF16),
        scratch=[
            pltpu.VMEM((sections, size, cols), BF16),
            pltpu.VMEM((sections * rank, part), BF16),
        ],
        specs=[SMEM] + [VMEM] * 9,
        name="sections",
    )(section_order, *all_sums, plain, *held)

    back = lax.all_to_all(
        results.reshape(sections * peers, block, cols),
        ("segment", "chip", "core"),
        split_axis=0,
        concat_axis=0,
        tiled=True,
    )
    rows = call(
        unpack_kernel,
        jax.ShapeDtypeStruct((count, width), BF16),
        specs=[VMEM, VMEM],
        name="unpack",
    )(homes[:, None], back.reshape(sections, size, cols))
    return rows[None]


def solution(mesh):
    planes, peers = mesh.devices.shape
    split = Mesh(mesh.devices.reshape(planes, peers // 2, 2), ("segment", "chip", "core"))
    rows = ("chip", "core")
    return jax.shard_map(
        local,
        mesh=split,
        in_specs=(
            P(rows, None),
            P(rows, None),
            P(),
            P("segment", None),
            P("segment", rows, None, None),
            P("segment", rows, None, None),
        ),
        out_specs=P("segment", rows, None),
        check_vma=False,
    )
```

```python
import jax
import jax.numpy as jnp
from jax import lax
from jax.experimental import pallas as pl
from jax.experimental.pallas import tpu as pltpu
from jax.sharding import Mesh
from jax.sharding import PartitionSpec as P

GROUPS = 4
FACTOR_FLOPS = 40_000_000_000
VMEM = pl.BlockSpec(memory_space=pltpu.VMEM)
ANY = pl.BlockSpec(memory_space=pl.ANY)
SMEM = pl.BlockSpec(memory_space=pltpu.SMEM)
F32 = jnp.float32
BF16 = jnp.bfloat16


def shifted(value, axis, steps):
    count = lax.axis_size(axis)
    return lax.ppermute(value, axis, [(source, (source + steps) % count) for source in range(count)])


def dot(a, b, contract_b=0, precision=None):
    return lax.dot_general(
        a, b, (((1,), (contract_b,)), ((), ())), precision=precision, preferred_element_type=F32
    )


def call(kernel, outs, *, scratch=(), flops=0, specs=None, room=48, **options):
    return pl.pallas_call(
        kernel,
        out_shape=outs,
        in_specs=specs,
        out_specs=jax.tree.map(lambda _: VMEM, outs),
        scratch_shapes=list(scratch),
        compiler_params=pltpu.CompilerParams(vmem_limit_bytes=room * 1024 * 1024),
        cost_estimate=pl.CostEstimate(flops=flops, bytes_accessed=4 << 20, transcendentals=0),
        **options,
    )


def one_hot(places, shape, axis):
    lines = lax.broadcasted_iota(jnp.int32, shape, axis)
    return jnp.where(lines == places, 1.0, 0.0).astype(BF16)


def block_places(shape, axis, count, core=None, only=None):
    line = lax.broadcasted_iota(jnp.int32, shape, axis)
    group = line // count
    row = line % count
    within = group * 2 + row % 2
    peer = row // 2
    if core is None:
        return peer * (2 * GROUPS) + within
    if only:
        return jnp.where(peer % 2 == core, peer * (2 * GROUPS) + within, -1)
    return jnp.where(peer % 2 == core, -1, (peer // 2) * (2 * GROUPS) + within)


def quarter_columns(plane, steps, part, planes=4):
    return pl.ds(pl.multiple_of(lax.rem(plane + steps, planes) * part, part), part)


def pack_kernel(places, hidden, out):
    cols = out.shape[1]
    chosen = one_hot(places[...], (out.shape[0], places.shape[1]), 0)
    stacked = jnp.concatenate(
        [hidden[:, g * cols : (g + 1) * cols] for g in range(GROUPS)], axis=0
    )
    out[...] = dot(chosen, stacked).astype(BF16)


def quarters_kernel(
    plane, shrink, gain, expand, q0, q1, q2, q3, taken, weights, gain_in, in_sem, put_sem
):
    rank = shrink.shape[0]
    outs = (q0, q1, q2, q3)
    part = q0.shape[1]
    columns = [
        pl.ds(pl.multiple_of(lax.rem(plane[0] + k, 4) * part, part), part) for k in range(4)
    ]
    load = pltpu.make_async_copy(gain, weights, gain_in)
    load.start()
    ins = [
        pltpu.make_async_copy(shrink.at[:, columns[k]], taken.at[k], in_sem.at[k])
        for k in range(4)
    ]
    puts = [
        pltpu.make_async_copy(
            expand.at[:, columns[k]], outs[k].at[pl.ds(rank, rank)], put_sem.at[k]
        )
        for k in range(4)
    ]
    for copy in ins + puts:
        copy.start()
    load.wait()
    for k in range(4):
        ins[k].wait()
        outs[k][:rank] = (taken[k].astype(F32) * weights[:, columns[k]]).astype(BF16)
    for copy in puts:
        copy.wait()


def factors_kernel(order, own, first, second, third, tiles, every, expand):
    pair = own.shape[0]
    rank = pair // 2
    for steps, ref in enumerate((own, first, second, third)):
        section = order[steps]
        every[pl.ds(pl.multiple_of(section * pair, pair), pair), :] = ref[...]
        expand[pl.ds(pl.multiple_of(section * rank, rank), rank), :] = ref[rank:]
    product = dot(expand[: 3 * rank], every[...], 1)

    def tile(row, section):
        return product[row * rank : (row + 1) * rank, section * pair : (section + 1) * pair]

    lanes = lax.broadcasted_iota(jnp.int32, (rank, pair), 1)

    def last(row):
        return jnp.where(lanes < rank, tile(row, 3), tile(row, row))

    for place, value in enumerate(
        (tile(0, 1), tile(0, 2), tile(1, 2), last(0), last(1), last(2))
    ):
        tiles[place * rank : (place + 1) * rank] = value


def rounded(value):
    high = value.astype(BF16)
    return high, value - high.astype(F32)


def products_kernel(
    order, blocks, others, tiles, own, first, second, third, sums, plain, product
):
    count, width = plain.shape
    cols = width // GROUPS
    size = count * GROUPS
    core = order[4]
    stacked = dot(
        one_hot(block_places((size, 1), 0, count, core, True), (size, blocks.shape[0]), 1),
        blocks[...],
    ) + dot(
        one_hot(block_places((size, 1), 0, count, core, False), (size, others.shape[0]), 1),
        others[...],
    )
    stacked = stacked.astype(BF16)
    for g in range(GROUPS):
        plain[:, g * cols : (g + 1) * cols] = stacked[g * count : (g + 1) * count]
    rows = plain[...]
    pair = own.shape[0]
    half = pair // 2
    for steps, ref in enumerate((own, first, second, third)):
        section = order[steps]
        product[:, pl.ds(pl.multiple_of(section * pair, pair), pair)] = dot(rows, ref[...], 1)
    values = rows.astype(F32)
    squares = jnp.sum(values * values, axis=1, keepdims=True)
    lanes = lax.broadcasted_iota(jnp.int32, (count, pair), 1)
    low = []
    for s in range(3):
        high, rest = rounded(product[:, s * pair : (s + 1) * pair])
        sums[:, s * pair : (s + 1) * pair] = high
        low.append(rest)
    high, rest = rounded(squares)
    ends = jnp.where(lanes < half, product[:, 3 * pair :], high.astype(F32))
    sums[:, 3 * pair : 4 * pair] = jnp.where(lanes < half + half // 2, ends, rest).astype(BF16)
    tile_low = []
    for at in range(3):
        high, rest = rounded(tiles[at * pair : (at + 1) * pair])
        sums[:, (6 + at) * pair : (7 + at) * pair] = high
        tile_low.append(rest)

    def both(left, right):
        return jnp.where(lanes < half, pltpu.roll(left, half, 1), right).astype(BF16)

    sums[:, 4 * pair : 5 * pair] = both(low[1], low[0])
    sums[:, 5 * pair : 6 * pair] = both(tile_low[2], low[2])
    sums[:, 9 * pair :] = both(tile_low[1], tile_low[0])


def sections_kernel(
    features, order, s0, s1, s2, s3, plain, f0, f1, f2, f3, out, stack, expand
):
    pair = f0.shape[0]
    rank = pair // 2
    count, width = plain.shape
    cols = width // GROUPS
    for steps, ref in enumerate((f0, f1, f2, f3)):
        section = order[steps]
        expand[pl.ds(pl.multiple_of(section * rank, rank), rank), :] = ref[rank:]
    lanes = lax.broadcasted_iota(jnp.int32, (count, pair), 1)

    def summed(at):
        columns = slice(at * pair, (at + 1) * pair)
        parts = [ref[:, columns].astype(F32) for ref in (s0, s1, s2, s3)]
        return (parts[0] + parts[1]) + (parts[2] + parts[3])

    def right(value):
        return jnp.where(lanes < rank, 0.0, value)

    def left(value):
        return right(pltpu.roll(value, rank, 1))

    low, mixed, tile_low = summed(4), summed(5), summed(9)
    y = [summed(0) + right(low), summed(1) + left(low), summed(2) + right(mixed), summed(3)]
    square = y[3][:, rank : rank + 1] + y[3][:, pair - 1 :]
    stacks = [summed(6) + right(tile_low), summed(7) + left(tile_low), summed(8) + left(mixed)]

    def thirds(place):
        at = (place % 2) * rank
        value = stacks[place // 2][at : at + rank]
        high, rest = rounded(value)
        middle, rest = rounded(rest)
        return jnp.concatenate([high, middle, rest.astype(BF16)], axis=0)

    uses = (((1, 0), (2, 1), (3, 3)), ((2, 2), (3, 4)), ((3, 5),))
    lowers = []
    for s in range(4):
        scale = lax.rsqrt(jnp.maximum(square, 0.0) / features + 1e-05)
        lower = (y[s][:, :rank] * scale).astype(BF16)
        lowers.append(lower)
        if s == 3:
            break
        added = dot(
            jnp.concatenate([lower] * 3, axis=1),
            jnp.concatenate([thirds(place) for _, place in uses[s]], axis=1),
        )
        value = lower.astype(F32)
        for at, (later, _) in enumerate(uses[s]):
            y[later] = y[later] + added[:, at * pair : (at + 1) * pair]
        ends = added[:, added.shape[1] - rank :]
        square = square + jnp.sum(value * (2.0 * y[s][:, rank:] + ends), axis=1, keepdims=True)
    for g in range(GROUPS):
        columns = slice(g * cols, (g + 1) * cols)
        current = plain[:, columns].astype(F32)
        for s in range(4):
            current = current + dot(lowers[s], expand[s * rank : (s + 1) * rank, columns])
            stack[s, g * count : (g + 1) * count] = current.astype(BF16)
    size = GROUPS * count
    moved = one_hot(block_places((1, size), 1, count), (size, size), 0)
    for s in range(4):
        out[s * size : (s + 1) * size] = dot(moved, stack[s]).astype(BF16)


def unpack_kernel(places, back, out):
    size, cols = places.shape[0], back.shape[2]
    count = size // GROUPS
    chosen = one_hot(places[...], (size, back.shape[1]), 1)
    for plane in range(back.shape[0]):
        found = dot(chosen, back[plane]).astype(BF16)
        for g in range(GROUPS):
            start = (plane * GROUPS + g) * cols
            out[:, start : start + cols] = found[g * count : (g + 1) * count]


def local(hidden_in, request_adapter, home_slot, gains, shrink_tiles, expand_tiles):
    chips = lax.axis_size("chip")
    peers = 2 * chips
    sections = lax.axis_size("segment")
    plane = lax.axis_index("segment")
    core = lax.axis_index("core")
    count, width = hidden_in.shape
    part = width // sections
    cols = part // GROUPS
    total = home_slot.shape[0]
    rank = expand_tiles.shape[2]
    pair = 2 * rank
    depth = 2
    block = depth * GROUPS
    size = peers * block

    quarters = call(
        quarters_kernel,
        tuple(jax.ShapeDtypeStruct((pair, part), BF16) for _ in range(sections)),
        scratch=[
            pltpu.VMEM((sections, rank, part), BF16),
            pltpu.VMEM((1, width), F32),
            pltpu.SemaphoreType.DMA,
            pltpu.SemaphoreType.DMA((sections,)),
            pltpu.SemaphoreType.DMA((sections,)),
        ],
        specs=[SMEM, ANY, ANY, ANY],
        room=60,
        name="quarters",
    )(plane.reshape(1), shrink_tiles[0, 0].T, gains, expand_tiles[0, 0])

    adapter_ids = request_adapter[:, 0]
    catalog = jnp.arange(total, dtype=jnp.int32)
    storage = jnp.sum(
        jnp.where(adapter_ids[:, None] == catalog[None, :], home_slot[None, :], 0), axis=1
    )
    order = jnp.arange(count, dtype=jnp.int32)
    same_adapter = adapter_ids[:, None] == adapter_ids[None, :]
    earlier = jnp.sum((same_adapter & (order[None, :] < order[:, None])).astype(jnp.int32), axis=1)
    groups = jnp.arange(GROUPS, dtype=jnp.int32)[:, None] * depth
    homes = (groups + (storage * block + earlier)[None, :]).reshape(-1)

    mine = lax.dynamic_slice(hidden_in, (0, plane * part), (count, part))
    packed = call(
        pack_kernel,
        jax.ShapeDtypeStruct((size, cols), BF16),
        specs=[VMEM, VMEM],
        name="pack",
    )(homes[None, :], mine)
    held = [quarters[0]] + [
        shifted(quarters[steps], "segment", steps) for steps in range(1, sections)
    ]

    arrived = lax.all_to_all(
        packed.reshape(chips, 2 * block, cols), "chip", split_axis=0, concat_axis=0, tiled=True
    )

    section_order = (plane - jnp.arange(sections, dtype=jnp.int32)) % sections
    section_order = jnp.concatenate([section_order, core.reshape(1)])
    tiles = call(
        factors_kernel,
        jax.ShapeDtypeStruct((6 * rank, pair), F32),
        scratch=[
            pltpu.VMEM((sections * pair, part), BF16),
            pltpu.VMEM((sections * rank, part), BF16),
        ],
        specs=[SMEM] + [VMEM] * 4,
        flops=FACTOR_FLOPS,
        name="factors",
    )(section_order, *held)
    arrived, tiles = lax.optimization_barrier((arrived, tiles))

    theirs = lax.dynamic_slice(arrived, (0, (1 - core) * block, 0), (chips, block, cols))
    others = lax.ppermute(theirs, "core", [(0, 1), (1, 0)]).reshape(chips * block, cols)
    sums, plain = call(
        products_kernel,
        (
            jax.ShapeDtypeStruct((peers * depth, 10 * pair), BF16),
            jax.ShapeDtypeStruct((peers * depth, part), BF16),
        ),
        scratch=[pltpu.VMEM((peers * depth, sections * pair), F32)],
        specs=[SMEM] + [VMEM] * 7,
        name="products",
    )(section_order, arrived.reshape(size, cols), others, tiles, *held)
    all_sums = [sums] + [shifted(sums, "segment", steps) for steps in range(1, sections)]

    results = call(
        lambda *refs: sections_kernel(width, *refs),
        jax.ShapeDtypeStruct((sections * size, cols), BF16),
        scratch=[
            pltpu.VMEM((sections, size, cols), BF16),
            pltpu.VMEM((sections * rank, part), BF16),
        ],
        specs=[SMEM] + [VMEM] * 9,
        name="sections",
    )(section_order, *all_sums, plain, *held)

    back = lax.all_to_all(
        results.reshape(sections * peers, block, cols),
        ("segment", "chip", "core"),
        split_axis=0,
        concat_axis=0,
        tiled=True,
    )
    rows = call(
        unpack_kernel,
        jax.ShapeDtypeStruct((count, width), BF16),
        specs=[VMEM, VMEM],
        name="unpack",
    )(homes[:, None], back.reshape(sections, size, cols))
    return rows[None]


def solution(mesh):
    planes, peers = mesh.devices.shape
    split = Mesh(mesh.devices.reshape(planes, peers // 2, 2), ("segment", "chip", "core"))
    rows = ("chip", "core")
    return jax.shard_map(
        local,
        mesh=split,
        in_specs=(
            P(rows, None),
            P(rows, None),
            P(),
            P("segment", None),
            P("segment", rows, None, None),
            P("segment", rows, None, None),
        ),
        out_specs=P("segment", rows, None),
        check_vma=False,
    )
```

```python
import jax
import jax.numpy as jnp
from jax import lax
from jax.experimental import pallas as pl
from jax.experimental.pallas import tpu as pltpu
from jax.sharding import Mesh
from jax.sharding import PartitionSpec as P

GROUPS = 4
FACTOR_FLOPS = 40_000_000_000
VMEM = pl.BlockSpec(memory_space=pltpu.VMEM)
ANY = pl.BlockSpec(memory_space=pl.ANY)
SMEM = pl.BlockSpec(memory_space=pltpu.SMEM)
F32 = jnp.float32
BF16 = jnp.bfloat16


def shifted(value, axis, steps):
    count = lax.axis_size(axis)
    return lax.ppermute(value, axis, [(source, (source + steps) % count) for source in range(count)])


def dot(a, b, contract_b=0, precision=None):
    return lax.dot_general(
        a, b, (((1,), (contract_b,)), ((), ())), precision=precision, preferred_element_type=F32
    )


def call(kernel, outs, *, scratch=(), flops=0, specs=None, out_spec=VMEM, room=48, **options):
    return pl.pallas_call(
        kernel,
        out_shape=outs,
        in_specs=specs,
        out_specs=jax.tree.map(lambda _: out_spec, outs),
        scratch_shapes=list(scratch),
        compiler_params=pltpu.CompilerParams(vmem_limit_bytes=room * 1024 * 1024),
        cost_estimate=pl.CostEstimate(flops=flops, bytes_accessed=4 << 20, transcendentals=0),
        **options,
    )


def one_hot(places, shape, axis):
    lines = lax.broadcasted_iota(jnp.int32, shape, axis)
    return jnp.where(lines == places, 1.0, 0.0).astype(BF16)


def block_places(shape, axis, count, core=None, only=None):
    line = lax.broadcasted_iota(jnp.int32, shape, axis)
    group = line // count
    row = line % count
    within = group * 2 + row % 2
    peer = row // 2
    if core is None:
        return peer * (2 * GROUPS) + within
    if only:
        return jnp.where(peer % 2 == core, peer * (2 * GROUPS) + within, -1)
    return jnp.where(peer % 2 == core, -1, (peer // 2) * (2 * GROUPS) + within)


def quarter_columns(plane, steps, part, planes=4):
    return pl.ds(pl.multiple_of(lax.rem(plane + steps, planes) * part, part), part)


def pack_kernel(places, hidden, out):
    cols = out.shape[1]
    chosen = one_hot(places[...], (out.shape[0], places.shape[1]), 0)
    stacked = jnp.concatenate(
        [hidden[:, g * cols : (g + 1) * cols] for g in range(GROUPS)], axis=0
    )
    out[...] = dot(chosen, stacked).astype(BF16)


def quarters_kernel(
    plane, shrink, gain, expand, q0, q1, q2, q3, taken, weights, gain_in, in_sem, put_sem
):
    rank = shrink.shape[0]
    outs = (q0, q1, q2, q3)
    part = q0.shape[1]
    columns = [
        pl.ds(pl.multiple_of(lax.rem(plane[0] + k, 4) * part, part), part) for k in range(4)
    ]
    load = pltpu.make_async_copy(gain, weights, gain_in)
    load.start()
    ins = [
        pltpu.make_async_copy(shrink.at[:, columns[k]], taken.at[k], in_sem.at[k])
        for k in range(4)
    ]
    puts = [
        pltpu.make_async_copy(
            expand.at[:, columns[k]], outs[k].at[pl.ds(rank, rank)], put_sem.at[k]
        )
        for k in range(4)
    ]
    for copy in ins + puts:
        copy.start()
    load.wait()
    for k in range(4):
        ins[k].wait()
        outs[k][:rank] = (taken[k].astype(F32) * weights[:, columns[k]]).astype(BF16)
    for copy in puts:
        copy.wait()


def ordered_copies(order, refs, first_row, rows, target, arrivals):
    copies = []
    for steps, ref in enumerate(refs):
        start = pl.multiple_of(order[steps] * rows, rows)
        copies.append(
            pltpu.make_async_copy(
                ref.at[pl.ds(first_row, rows)], target.at[pl.ds(start, rows)], arrivals.at[steps]
            )
        )
        copies[-1].start()
    return copies


def factors_kernel(order, own, first, second, third, tiles, every, expand, every_in, expand_in):
    pair = own.shape[0]
    rank = pair // 2
    refs = (own, first, second, third)
    copies = ordered_copies(order, refs, 0, pair, every, every_in)
    copies += ordered_copies(order, refs, rank, rank, expand, expand_in)
    for copy in copies:
        copy.wait()
    product = dot(expand[: 3 * rank], every[...], 1)

    def tile(row, section):
        return product[row * rank : (row + 1) * rank, section * pair : (section + 1) * pair]

    lanes = lax.broadcasted_iota(jnp.int32, (rank, pair), 1)

    def last(row):
        return jnp.where(lanes < rank, tile(row, 3), tile(row, row))

    for place, value in enumerate(
        (tile(0, 1), tile(0, 2), tile(1, 2), last(0), last(1), last(2))
    ):
        tiles[place * rank : (place + 1) * rank] = value


def rounded(value):
    high = value.astype(BF16)
    return high, value - high.astype(F32)


def plain_kernel(core, blocks, others, plain, squares):
    count, width = plain.shape
    cols = width // GROUPS
    size = count * GROUPS
    stacked = dot(
        one_hot(block_places((size, 1), 0, count, core[0], True), (size, blocks.shape[0]), 1),
        blocks[...],
    ) + dot(
        one_hot(block_places((size, 1), 0, count, core[0], False), (size, others.shape[0]), 1),
        others[...],
    )
    total = jnp.zeros((count, 1), F32)
    for g in range(GROUPS):
        rows = stacked[g * count : (g + 1) * count]
        plain[:, g * cols : (g + 1) * cols] = rows.astype(BF16)
        total = total + jnp.sum(rows * rows, axis=1, keepdims=True)
    squares[...] = jnp.broadcast_to(total, squares.shape)


def products_kernel(
    order, plain, squares, tiles, own, first, second, third, sums, product
):
    count = plain.shape[0]
    rows = plain[...]
    pair = own.shape[0]
    half = pair // 2
    for steps, ref in enumerate((own, first, second, third)):
        section = order[steps]
        product[:, pl.ds(pl.multiple_of(section * pair, pair), pair)] = dot(rows, ref[...], 1)
    lanes = lax.broadcasted_iota(jnp.int32, (count, pair), 1)
    low = []
    for s in range(3):
        high, rest = rounded(product[:, s * pair : (s + 1) * pair])
        sums[:, s * pair : (s + 1) * pair] = high
        low.append(rest)
    high, rest = rounded(squares[...])
    ends = jnp.where(lanes < half, product[:, 3 * pair :], high.astype(F32))
    sums[:, 3 * pair : 4 * pair] = jnp.where(lanes < half + half // 2, ends, rest).astype(BF16)
    tile_low = []
    for at in range(3):
        high, rest = rounded(tiles[at * pair : (at + 1) * pair])
        sums[:, (6 + at) * pair : (7 + at) * pair] = high
        tile_low.append(rest)

    def both(left, right):
        return jnp.where(lanes < half, pltpu.roll(left, half, 1), right).astype(BF16)

    sums[:, 4 * pair : 5 * pair] = both(low[1], low[0])
    sums[:, 5 * pair : 6 * pair] = both(tile_low[2], low[2])
    sums[:, 9 * pair :] = both(tile_low[1], tile_low[0])


def sections_kernel(
    features, order, s0, s1, s2, s3, plain_ref, f0, f1, f2, f3, out,
    stack, expand, plain, made, expand_in, plain_in, sent
):
    pair = f0.shape[0]
    rank = pair // 2
    count, width = plain.shape
    cols = width // GROUPS
    copies = ordered_copies(order, (f0, f1, f2, f3), rank, rank, expand, expand_in)
    copies.append(pltpu.make_async_copy(plain_ref, plain, plain_in))
    copies[-1].start()
    lanes = lax.broadcasted_iota(jnp.int32, (count, pair), 1)

    def summed(at):
        columns = slice(at * pair, (at + 1) * pair)
        parts = [ref[:, columns].astype(F32) for ref in (s0, s1, s2, s3)]
        return (parts[0] + parts[1]) + (parts[2] + parts[3])

    def right(value):
        return jnp.where(lanes < rank, 0.0, value)

    def left(value):
        return right(pltpu.roll(value, rank, 1))

    low, mixed, tile_low = summed(4), summed(5), summed(9)
    y = [summed(0) + right(low), summed(1) + left(low), summed(2) + right(mixed), summed(3)]
    square = y[3][:, rank : rank + 1] + y[3][:, pair - 1 :]
    stacks = [summed(6) + right(tile_low), summed(7) + left(tile_low), summed(8) + left(mixed)]

    def thirds(place):
        at = (place % 2) * rank
        value = stacks[place // 2][at : at + rank]
        high, rest = rounded(value)
        middle, rest = rounded(rest)
        return jnp.concatenate([high, middle, rest.astype(BF16)], axis=0)

    uses = (((1, 0), (2, 1), (3, 3)), ((2, 2), (3, 4)), ((3, 5),))
    lowers = []
    for s in range(4):
        scale = lax.rsqrt(jnp.maximum(square, 0.0) / features + 1e-05)
        lower = (y[s][:, :rank] * scale).astype(BF16)
        lowers.append(lower)
        if s == 3:
            break
        added = dot(
            jnp.concatenate([lower] * 3, axis=1),
            jnp.concatenate([thirds(place) for _, place in uses[s]], axis=1),
        )
        value = lower.astype(F32)
        for at, (later, _) in enumerate(uses[s]):
            y[later] = y[later] + added[:, at * pair : (at + 1) * pair]
        ends = added[:, added.shape[1] - rank :]
        square = square + jnp.sum(value * (2.0 * y[s][:, rank:] + ends), axis=1, keepdims=True)
    size = GROUPS * count
    moved = one_hot(block_places((1, size), 1, count), (size, size), 0)
    for copy in copies:
        copy.wait()
    current = [plain[:, g * cols : (g + 1) * cols].astype(F32) for g in range(GROUPS)]
    sends = []
    for s in range(4):
        for g in range(GROUPS):
            columns = slice(g * cols, (g + 1) * cols)
            current[g] = current[g] + dot(lowers[s], expand[s * rank : (s + 1) * rank, columns])
            stack[s, g * count : (g + 1) * count] = current[g].astype(BF16)
        made[s] = dot(moved, stack[s]).astype(BF16)
        sends.append(
            pltpu.make_async_copy(made.at[s], out.at[pl.ds(s * size, size)], sent.at[s])
        )
        sends[-1].start()
    for copy in sends:
        copy.wait()


def unpack_kernel(places, back, out):
    size, cols = places.shape[0], back.shape[2]
    count = size // GROUPS
    chosen = one_hot(places[...], (size, back.shape[1]), 1)
    for plane in range(back.shape[0]):
        found = dot(chosen, back[plane]).astype(BF16)
        for g in range(GROUPS):
            start = (plane * GROUPS + g) * cols
            out[:, start : start + cols] = found[g * count : (g + 1) * count]


def local(hidden_in, request_adapter, home_slot, gains, shrink_tiles, expand_tiles):
    chips = lax.axis_size("chip")
    peers = 2 * chips
    sections = lax.axis_size("segment")
    plane = lax.axis_index("segment")
    core = lax.axis_index("core")
    count, width = hidden_in.shape
    part = width // sections
    cols = part // GROUPS
    total = home_slot.shape[0]
    rank = expand_tiles.shape[2]
    pair = 2 * rank
    depth = 2
    block = depth * GROUPS
    size = peers * block

    quarters = call(
        quarters_kernel,
        tuple(jax.ShapeDtypeStruct((pair, part), BF16) for _ in range(sections)),
        scratch=[
            pltpu.VMEM((sections, rank, part), BF16),
            pltpu.VMEM((1, width), F32),
            pltpu.SemaphoreType.DMA,
            pltpu.SemaphoreType.DMA((sections,)),
            pltpu.SemaphoreType.DMA((sections,)),
        ],
        specs=[SMEM, ANY, ANY, ANY],
        room=60,
        name="quarters",
    )(plane.reshape(1), shrink_tiles[0, 0].T, gains, expand_tiles[0, 0])

    adapter_ids = request_adapter[:, 0]
    catalog = jnp.arange(total, dtype=jnp.int32)
    storage = jnp.sum(
        jnp.where(adapter_ids[:, None] == catalog[None, :], home_slot[None, :], 0), axis=1
    )
    order = jnp.arange(count, dtype=jnp.int32)
    same_adapter = adapter_ids[:, None] == adapter_ids[None, :]
    earlier = jnp.sum((same_adapter & (order[None, :] < order[:, None])).astype(jnp.int32), axis=1)
    groups = jnp.arange(GROUPS, dtype=jnp.int32)[:, None] * depth
    homes = (groups + (storage * block + earlier)[None, :]).reshape(-1)

    mine = lax.dynamic_slice(hidden_in, (0, plane * part), (count, part))
    packed = call(
        pack_kernel,
        jax.ShapeDtypeStruct((size, cols), BF16),
        specs=[VMEM, VMEM],
        name="pack",
    )(homes[None, :], mine)
    held = [quarters[0]] + [
        shifted(quarters[steps], "segment", steps) for steps in range(1, sections)
    ]

    arrived = lax.all_to_all(
        packed.reshape(chips, 2 * block, cols), "chip", split_axis=0, concat_axis=0, tiled=True
    )

    section_order = (plane - jnp.arange(sections, dtype=jnp.int32)) % sections
    tiles = call(
        factors_kernel,
        jax.ShapeDtypeStruct((6 * rank, pair), F32),
        scratch=[
            pltpu.VMEM((sections * pair, part), BF16),
            pltpu.VMEM((sections * rank, part), BF16),
            pltpu.SemaphoreType.DMA((sections,)),
            pltpu.SemaphoreType.DMA((sections,)),
        ],
        specs=[SMEM] + [ANY] * 4,
        flops=FACTOR_FLOPS,
        name="factors",
    )(section_order, *held)
    arrived, tiles = lax.optimization_barrier((arrived, tiles))
    theirs = lax.dynamic_slice(arrived, (0, (1 - core) * block, 0), (chips, block, cols))
    others = lax.ppermute(theirs, "core", [(0, 1), (1, 0)]).reshape(chips * block, cols)
    plain, squares = call(
        plain_kernel,
        (
            jax.ShapeDtypeStruct((peers * depth, part), BF16),
            jax.ShapeDtypeStruct((peers * depth, pair), F32),
        ),
        specs=[SMEM] + [VMEM] * 2,
        name="plain",
    )(core.reshape(1), arrived.reshape(size, cols), others)
    sums = call(
        products_kernel,
        jax.ShapeDtypeStruct((peers * depth, 10 * pair), BF16),
        scratch=[pltpu.VMEM((peers * depth, sections * pair), F32)],
        specs=[SMEM] + [VMEM] * 7,
        name="products",
    )(section_order, plain, squares, tiles, *held)
    all_sums = [sums] + [shifted(sums, "segment", steps) for steps in range(1, sections)]

    results = call(
        lambda *refs: sections_kernel(width, *refs),
        jax.ShapeDtypeStruct((sections * size, cols), BF16),
        scratch=[
            pltpu.VMEM((sections, size, cols), BF16),
            pltpu.VMEM((sections * rank, part), BF16),
            pltpu.VMEM((peers * depth, part), BF16),
            pltpu.VMEM((sections, size, cols), BF16),
            pltpu.SemaphoreType.DMA((sections,)),
            pltpu.SemaphoreType.DMA,
            pltpu.SemaphoreType.DMA((sections,)),
        ],
        specs=[SMEM] + [VMEM] * 4 + [ANY] * 5,
        out_spec=ANY,
        name="sections",
    )(section_order, *all_sums, plain, *held)

    back = lax.all_to_all(
        results.reshape(sections * peers, block, cols),
        ("segment", "chip", "core"),
        split_axis=0,
        concat_axis=0,
        tiled=True,
    )
    rows = call(
        unpack_kernel,
        jax.ShapeDtypeStruct((count, width), BF16),
        specs=[VMEM, VMEM],
        name="unpack",
    )(homes[:, None], back.reshape(sections, size, cols))
    return rows[None]


def solution(mesh):
    planes, peers = mesh.devices.shape
    split = Mesh(mesh.devices.reshape(planes, peers // 2, 2), ("segment", "chip", "core"))
    rows = ("chip", "core")
    return jax.shard_map(
        local,
        mesh=split,
        in_specs=(
            P(rows, None),
            P(rows, None),
            P(),
            P("segment", None),
            P("segment", rows, None, None),
            P("segment", rows, None, None),
        ),
        out_specs=P("segment", rows, None),
        check_vma=False,
    )
```

```python
import jax
import jax.numpy as jnp
from jax import lax
from jax.experimental import pallas as pl
from jax.experimental.pallas import tpu as pltpu
from jax.sharding import Mesh
from jax.sharding import PartitionSpec as P

GROUPS = 4
FACTOR_FLOPS = 40_000_000_000
VMEM = pl.BlockSpec(memory_space=pltpu.VMEM)
ANY = pl.BlockSpec(memory_space=pl.ANY)
SMEM = pl.BlockSpec(memory_space=pltpu.SMEM)
F32 = jnp.float32
BF16 = jnp.bfloat16


def shifted(value, axis, steps):
    count = lax.axis_size(axis)
    return lax.ppermute(value, axis, [(source, (source + steps) % count) for source in range(count)])


def dot(a, b, contract_b=0, precision=None):
    return lax.dot_general(
        a, b, (((1,), (contract_b,)), ((), ())), precision=precision, preferred_element_type=F32
    )


def call(kernel, outs, *, scratch=(), flops=0, specs=None, out_spec=VMEM, room=48, **options):
    return pl.pallas_call(
        kernel,
        out_shape=outs,
        in_specs=specs,
        out_specs=jax.tree.map(lambda _: out_spec, outs),
        scratch_shapes=list(scratch),
        compiler_params=pltpu.CompilerParams(vmem_limit_bytes=room * 1024 * 1024),
        cost_estimate=pl.CostEstimate(flops=flops, bytes_accessed=4 << 20, transcendentals=0),
        **options,
    )


def one_hot(places, shape, axis):
    lines = lax.broadcasted_iota(jnp.int32, shape, axis)
    return jnp.where(lines == places, 1.0, 0.0).astype(BF16)


def block_places(shape, axis, count, core=None, only=None):
    line = lax.broadcasted_iota(jnp.int32, shape, axis)
    group = line // count
    row = line % count
    within = group * 2 + row % 2
    peer = row // 2
    if core is None:
        return peer * (2 * GROUPS) + within
    if only:
        return jnp.where(peer % 2 == core, peer * (2 * GROUPS) + within, -1)
    return jnp.where(peer % 2 == core, -1, (peer // 2) * (2 * GROUPS) + within)


def quarter_columns(plane, steps, part, planes=4):
    return pl.ds(pl.multiple_of(lax.rem(plane + steps, planes) * part, part), part)


def pack_kernel(places, hidden, out):
    cols = out.shape[1]
    chosen = one_hot(places[...], (out.shape[0], places.shape[1]), 0)
    stacked = jnp.concatenate(
        [hidden[:, g * cols : (g + 1) * cols] for g in range(GROUPS)], axis=0
    )
    out[...] = dot(chosen, stacked).astype(BF16)


def quarters_kernel(shifts, plane, shrink, gain, expand, *refs):
    number = len(shifts)
    outs = refs[:number]
    taken, weights, gain_in, in_sem, put_sem = refs[number:]
    rank = shrink.shape[0]
    part = outs[0].shape[1]
    columns = [
        pl.ds(pl.multiple_of(lax.rem(plane[0] + k, 4) * part, part), part) for k in shifts
    ]
    loads, ins, puts = [], [], []
    for at in range(number):
        loads.append(
            pltpu.make_async_copy(gain.at[:, columns[at]], weights.at[at], gain_in.at[at])
        )
        ins.append(pltpu.make_async_copy(shrink.at[:, columns[at]], taken.at[at], in_sem.at[at]))
        puts.append(
            pltpu.make_async_copy(
                expand.at[:, columns[at]], outs[at].at[pl.ds(rank, rank)], put_sem.at[at]
            )
        )
    for copy in loads + ins + puts:
        copy.start()
    for at in range(number):
        loads[at].wait()
        ins[at].wait()
        outs[at][:rank] = (taken[at].astype(F32) * weights[at]).astype(BF16)
    for copy in puts:
        copy.wait()


def factors_kernel(order, own, first, second, third, tiles, every, expand):
    pair = own.shape[0]
    rank = pair // 2
    for steps, ref in enumerate((own, first, second, third)):
        section = order[steps]
        every[pl.ds(pl.multiple_of(section * pair, pair), pair), :] = ref[...]
        expand[pl.ds(pl.multiple_of(section * rank, rank), rank), :] = ref[rank:]
    product = dot(expand[: 3 * rank], every[...], 1)

    def tile(row, section):
        return product[row * rank : (row + 1) * rank, section * pair : (section + 1) * pair]

    lanes = lax.broadcasted_iota(jnp.int32, (rank, pair), 1)

    def last(row):
        return jnp.where(lanes < rank, tile(row, 3), tile(row, row))

    for place, value in enumerate(
        (tile(0, 1), tile(0, 2), tile(1, 2), last(0), last(1), last(2))
    ):
        tiles[place * rank : (place + 1) * rank] = value


def rounded(value):
    high = value.astype(BF16)
    return high, value - high.astype(F32)


def products_kernel(
    order, blocks, others, tiles, own, first, second, third, sums, plain, product
):
    count, width = plain.shape
    cols = width // GROUPS
    size = count * GROUPS
    core = order[4]
    stacked = dot(
        one_hot(block_places((size, 1), 0, count, core, True), (size, blocks.shape[0]), 1),
        blocks[...],
    ) + dot(
        one_hot(block_places((size, 1), 0, count, core, False), (size, others.shape[0]), 1),
        others[...],
    )
    stacked = stacked.astype(BF16)
    for g in range(GROUPS):
        plain[:, g * cols : (g + 1) * cols] = stacked[g * count : (g + 1) * count]
    rows = plain[...]
    pair = own.shape[0]
    half = pair // 2
    for steps, ref in enumerate((own, first, second, third)):
        section = order[steps]
        product[:, pl.ds(pl.multiple_of(section * pair, pair), pair)] = dot(rows, ref[...], 1)
    values = rows.astype(F32)
    squares = jnp.sum(values * values, axis=1, keepdims=True)
    lanes = lax.broadcasted_iota(jnp.int32, (count, pair), 1)
    low = []
    for s in range(3):
        high, rest = rounded(product[:, s * pair : (s + 1) * pair])
        sums[:, s * pair : (s + 1) * pair] = high
        low.append(rest)
    high, rest = rounded(squares)
    ends = jnp.where(lanes < half, product[:, 3 * pair :], high.astype(F32))
    sums[:, 3 * pair : 4 * pair] = jnp.where(lanes < half + half // 2, ends, rest).astype(BF16)
    tile_low = []
    for at in range(3):
        high, rest = rounded(tiles[at * pair : (at + 1) * pair])
        sums[:, (6 + at) * pair : (7 + at) * pair] = high
        tile_low.append(rest)

    def both(left, right):
        return jnp.where(lanes < half, pltpu.roll(left, half, 1), right).astype(BF16)

    sums[:, 4 * pair : 5 * pair] = both(low[1], low[0])
    sums[:, 5 * pair : 6 * pair] = both(tile_low[2], low[2])
    sums[:, 9 * pair :] = both(tile_low[1], tile_low[0])


def sections_kernel(
    features, order, s0, s1, s2, s3, plain, f0, f1, f2, f3, out, stack, expand, made, sent
):
    pair = f0.shape[0]
    rank = pair // 2
    count, width = plain.shape
    cols = width // GROUPS
    for steps, ref in enumerate((f0, f1, f2, f3)):
        section = order[steps]
        expand[pl.ds(pl.multiple_of(section * rank, rank), rank), :] = ref[rank:]
    lanes = lax.broadcasted_iota(jnp.int32, (count, pair), 1)

    def summed(at):
        columns = slice(at * pair, (at + 1) * pair)
        parts = [ref[:, columns].astype(F32) for ref in (s0, s1, s2, s3)]
        return (parts[0] + parts[1]) + (parts[2] + parts[3])

    def right(value):
        return jnp.where(lanes < rank, 0.0, value)

    def left(value):
        return right(pltpu.roll(value, rank, 1))

    low, mixed, tile_low = summed(4), summed(5), summed(9)
    y = [summed(0) + right(low), summed(1) + left(low), summed(2) + right(mixed), summed(3)]
    square = y[3][:, rank : rank + 1] + y[3][:, pair - 1 :]
    stacks = [summed(6) + right(tile_low), summed(7) + left(tile_low), summed(8) + left(mixed)]

    def thirds(place):
        at = (place % 2) * rank
        value = stacks[place // 2][at : at + rank]
        high, rest = rounded(value)
        middle, rest = rounded(rest)
        return jnp.concatenate([high, middle, rest.astype(BF16)], axis=0)

    uses = (((1, 0), (2, 1), (3, 3)), ((2, 2), (3, 4)), ((3, 5),))
    lowers = []
    for s in range(4):
        scale = lax.rsqrt(jnp.maximum(square, 0.0) / features + 1e-05)
        lower = (y[s][:, :rank] * scale).astype(BF16)
        lowers.append(lower)
        if s == 3:
            break
        added = dot(
            jnp.concatenate([lower] * 3, axis=1),
            jnp.concatenate([thirds(place) for _, place in uses[s]], axis=1),
        )
        value = lower.astype(F32)
        for at, (later, _) in enumerate(uses[s]):
            y[later] = y[later] + added[:, at * pair : (at + 1) * pair]
        ends = added[:, added.shape[1] - rank :]
        square = square + jnp.sum(value * (2.0 * y[s][:, rank:] + ends), axis=1, keepdims=True)
    size = GROUPS * count
    moved = one_hot(block_places((1, size), 1, count), (size, size), 0)
    current = [plain[:, g * cols : (g + 1) * cols].astype(F32) for g in range(GROUPS)]
    sends = []
    for s in range(4):
        for g in range(GROUPS):
            columns = slice(g * cols, (g + 1) * cols)
            current[g] = current[g] + dot(lowers[s], expand[s * rank : (s + 1) * rank, columns])
            stack[s, g * count : (g + 1) * count] = current[g].astype(BF16)
        made[s] = dot(moved, stack[s]).astype(BF16)
        sends.append(
            pltpu.make_async_copy(made.at[s], out.at[pl.ds(s * size, size)], sent.at[s])
        )
        sends[-1].start()
    for copy in sends:
        copy.wait()


def unpack_kernel(places, back, out):
    size, cols = places.shape[0], back.shape[2]
    count = size // GROUPS
    chosen = one_hot(places[...], (size, back.shape[1]), 1)
    for plane in range(back.shape[0]):
        found = dot(chosen, back[plane]).astype(BF16)
        for g in range(GROUPS):
            start = (plane * GROUPS + g) * cols
            out[:, start : start + cols] = found[g * count : (g + 1) * count]


def local(hidden_in, request_adapter, home_slot, gains, shrink_tiles, expand_tiles):
    chips = lax.axis_size("chip")
    peers = 2 * chips
    sections = lax.axis_size("segment")
    plane = lax.axis_index("segment")
    core = lax.axis_index("core")
    count, width = hidden_in.shape
    part = width // sections
    cols = part // GROUPS
    total = home_slot.shape[0]
    rank = expand_tiles.shape[2]
    pair = 2 * rank
    depth = 2
    block = depth * GROUPS
    size = peers * block

    def quarters_of(*shifts):
        number = len(shifts)
        return call(
            lambda *refs: quarters_kernel(shifts, *refs),
            tuple(jax.ShapeDtypeStruct((pair, part), BF16) for _ in shifts),
            scratch=[
                pltpu.VMEM((number, rank, part), BF16),
                pltpu.VMEM((number, 1, part), F32),
                pltpu.SemaphoreType.DMA((number,)),
                pltpu.SemaphoreType.DMA((number,)),
                pltpu.SemaphoreType.DMA((number,)),
            ],
            specs=[SMEM, ANY, ANY, ANY],
            room=60,
            name="quarters",
        )(plane.reshape(1), shrink_tiles[0, 0].T, gains, expand_tiles[0, 0])

    near, behind = quarters_of(1, 3)
    far, kept = quarters_of(2, 0)

    adapter_ids = request_adapter[:, 0]
    catalog = jnp.arange(total, dtype=jnp.int32)
    storage = jnp.sum(
        jnp.where(adapter_ids[:, None] == catalog[None, :], home_slot[None, :], 0), axis=1
    )
    order = jnp.arange(count, dtype=jnp.int32)
    same_adapter = adapter_ids[:, None] == adapter_ids[None, :]
    earlier = jnp.sum((same_adapter & (order[None, :] < order[:, None])).astype(jnp.int32), axis=1)
    groups = jnp.arange(GROUPS, dtype=jnp.int32)[:, None] * depth
    homes = (groups + (storage * block + earlier)[None, :]).reshape(-1)

    mine = lax.dynamic_slice(hidden_in, (0, plane * part), (count, part))
    packed = call(
        pack_kernel,
        jax.ShapeDtypeStruct((size, cols), BF16),
        specs=[VMEM, VMEM],
        name="pack",
    )(homes[None, :], mine)
    sent = ((1, near), (2, far), (3, behind))
    held = [kept] + [shifted(quarter, "segment", steps) for steps, quarter in sent]

    arrived = lax.all_to_all(
        packed.reshape(chips, 2 * block, cols), "chip", split_axis=0, concat_axis=0, tiled=True
    )

    section_order = (plane - jnp.arange(sections, dtype=jnp.int32)) % sections
    section_order = jnp.concatenate([section_order, core.reshape(1)])
    tiles = call(
        factors_kernel,
        jax.ShapeDtypeStruct((6 * rank, pair), F32),
        scratch=[
            pltpu.VMEM((sections * pair, part), BF16),
            pltpu.VMEM((sections * rank, part), BF16),
        ],
        specs=[SMEM] + [VMEM] * 4,
        flops=FACTOR_FLOPS,
        name="factors",
    )(section_order, *held)
    arrived, tiles = lax.optimization_barrier((arrived, tiles))

    theirs = lax.dynamic_slice(arrived, (0, (1 - core) * block, 0), (chips, block, cols))
    others = lax.ppermute(theirs, "core", [(0, 1), (1, 0)]).reshape(chips * block, cols)
    sums, plain = call(
        products_kernel,
        (
            jax.ShapeDtypeStruct((peers * depth, 10 * pair), BF16),
            jax.ShapeDtypeStruct((peers * depth, part), BF16),
        ),
        scratch=[pltpu.VMEM((peers * depth, sections * pair), F32)],
        specs=[SMEM] + [VMEM] * 7,
        name="products",
    )(section_order, arrived.reshape(size, cols), others, tiles, *held)
    all_sums = [sums] + [shifted(sums, "segment", steps) for steps in range(1, sections)]

    results = call(
        lambda *refs: sections_kernel(width, *refs),
        jax.ShapeDtypeStruct((sections * size, cols), BF16),
        scratch=[
            pltpu.VMEM((sections, size, cols), BF16),
            pltpu.VMEM((sections * rank, part), BF16),
            pltpu.VMEM((sections, size, cols), BF16),
            pltpu.SemaphoreType.DMA((sections,)),
        ],
        specs=[SMEM] + [VMEM] * 9,
        out_spec=ANY,
        name="sections",
    )(section_order, *all_sums, plain, *held)

    back = lax.all_to_all(
        results.reshape(sections * peers, block, cols),
        ("segment", "chip", "core"),
        split_axis=0,
        concat_axis=0,
        tiled=True,
    )
    rows = call(
        unpack_kernel,
        jax.ShapeDtypeStruct((count, width), BF16),
        specs=[VMEM, VMEM],
        name="unpack",
    )(homes[:, None], back.reshape(sections, size, cols))
    return rows[None]


def solution(mesh):
    planes, peers = mesh.devices.shape
    split = Mesh(mesh.devices.reshape(planes, peers // 2, 2), ("segment", "chip", "core"))
    rows = ("chip", "core")
    return jax.shard_map(
        local,
        mesh=split,
        in_specs=(
            P(rows, None),
            P(rows, None),
            P(),
            P("segment", None),
            P("segment", rows, None, None),
            P("segment", rows, None, None),
        ),
        out_specs=P("segment", rows, None),
        check_vma=False,
    )
```

```python
import jax
import jax.numpy as jnp
from jax import lax
from jax.experimental import pallas as pl
from jax.experimental.pallas import tpu as pltpu
from jax.sharding import Mesh
from jax.sharding import PartitionSpec as P

GROUPS = 4
FACTOR_FLOPS = 40_000_000_000
VMEM = pl.BlockSpec(memory_space=pltpu.VMEM)
ANY = pl.BlockSpec(memory_space=pl.ANY)
SMEM = pl.BlockSpec(memory_space=pltpu.SMEM)
F32 = jnp.float32
BF16 = jnp.bfloat16


def shifted(value, axis, steps):
    count = lax.axis_size(axis)
    return lax.ppermute(value, axis, [(source, (source + steps) % count) for source in range(count)])


def dot(a, b, contract_b=0, precision=None):
    return lax.dot_general(
        a, b, (((1,), (contract_b,)), ((), ())), precision=precision, preferred_element_type=F32
    )


def call(kernel, outs, *, scratch=(), flops=0, specs=None, out_spec=VMEM, room=48, **options):
    return pl.pallas_call(
        kernel,
        out_shape=outs,
        in_specs=specs,
        out_specs=jax.tree.map(lambda _: out_spec, outs),
        scratch_shapes=list(scratch),
        compiler_params=pltpu.CompilerParams(vmem_limit_bytes=room * 1024 * 1024),
        cost_estimate=pl.CostEstimate(flops=flops, bytes_accessed=4 << 20, transcendentals=0),
        **options,
    )


def one_hot(places, shape, axis):
    lines = lax.broadcasted_iota(jnp.int32, shape, axis)
    return jnp.where(lines == places, 1.0, 0.0).astype(BF16)


def block_places(shape, axis, count, core=None, only=None):
    line = lax.broadcasted_iota(jnp.int32, shape, axis)
    group = line // count
    row = line % count
    within = group * 2 + row % 2
    peer = row // 2
    if core is None:
        return peer * (2 * GROUPS) + within
    if only:
        return jnp.where(peer % 2 == core, peer * (2 * GROUPS) + within, -1)
    return jnp.where(peer % 2 == core, -1, (peer // 2) * (2 * GROUPS) + within)


def quarter_columns(plane, steps, part, planes=4):
    return pl.ds(pl.multiple_of(lax.rem(plane + steps, planes) * part, part), part)


def pack_kernel(places, hidden, out):
    cols = out.shape[1]
    chosen = one_hot(places[...], (out.shape[0], places.shape[1]), 0)
    stacked = jnp.concatenate(
        [hidden[:, g * cols : (g + 1) * cols] for g in range(GROUPS)], axis=0
    )
    out[...] = dot(chosen, stacked).astype(BF16)


def quarters_kernel(
    plane, shrink, gain, expand, q0, q1, q2, q3, taken, weights, gain_in, in_sem, put_sem
):
    rank = shrink.shape[0]
    outs = (q0, q1, q2, q3)
    part = q0.shape[1]
    columns = [
        pl.ds(pl.multiple_of(lax.rem(plane[0] + k, 4) * part, part), part) for k in range(4)
    ]
    load = pltpu.make_async_copy(gain, weights, gain_in)
    load.start()
    ins = [
        pltpu.make_async_copy(shrink.at[:, columns[k]], taken.at[k], in_sem.at[k])
        for k in range(4)
    ]
    puts = [
        pltpu.make_async_copy(
            expand.at[:, columns[k]], outs[k].at[pl.ds(rank, rank)], put_sem.at[k]
        )
        for k in range(4)
    ]
    for copy in ins + puts:
        copy.start()
    load.wait()
    for k in range(4):
        ins[k].wait()
        outs[k][:rank] = (taken[k].astype(F32) * weights[:, columns[k]]).astype(BF16)
    for copy in puts:
        copy.wait()


def factors_kernel(order, own, first, second, third, tiles, every, expand):
    pair = own.shape[0]
    rank = pair // 2
    for steps, ref in enumerate((own, first, second, third)):
        section = order[steps]
        every[pl.ds(pl.multiple_of(section * pair, pair), pair), :] = ref[...]
        expand[pl.ds(pl.multiple_of(section * rank, rank), rank), :] = ref[rank:]
    product = dot(expand[: 3 * rank], every[...], 1)

    def tile(row, section):
        return product[row * rank : (row + 1) * rank, section * pair : (section + 1) * pair]

    lanes = lax.broadcasted_iota(jnp.int32, (rank, pair), 1)

    def last(row):
        return jnp.where(lanes < rank, tile(row, 3), tile(row, row))

    for place, value in enumerate(
        (tile(0, 1), tile(0, 2), tile(1, 2), last(0), last(1), last(2))
    ):
        tiles[place * rank : (place + 1) * rank] = value


def rounded(value):
    high = value.astype(BF16)
    return high, value - high.astype(F32)


def products_kernel(
    order, blocks, others, tiles, own, first, second, third, sums, plain, product
):
    count, width = plain.shape
    cols = width // GROUPS
    size = count * GROUPS
    core = order[4]
    stacked = dot(
        one_hot(block_places((size, 1), 0, count, core, True), (size, blocks.shape[0]), 1),
        blocks[...],
    ) + dot(
        one_hot(block_places((size, 1), 0, count, core, False), (size, others.shape[0]), 1),
        others[...],
    )
    stacked = stacked.astype(BF16)
    for g in range(GROUPS):
        plain[:, g * cols : (g + 1) * cols] = stacked[g * count : (g + 1) * count]
    rows = plain[...]
    pair = own.shape[0]
    half = pair // 2
    for steps, ref in enumerate((own, first, second, third)):
        section = order[steps]
        product[:, pl.ds(pl.multiple_of(section * pair, pair), pair)] = dot(rows, ref[...], 1)
    values = rows.astype(F32)
    squares = jnp.sum(values * values, axis=1, keepdims=True)
    lanes = lax.broadcasted_iota(jnp.int32, (count, pair), 1)
    sums[:, : 3 * pair] = product[:, : 3 * pair].astype(BF16)
    high, rest = rounded(squares)
    ends = jnp.where(lanes < half, product[:, 3 * pair :], high.astype(F32))
    sums[:, 3 * pair : 4 * pair] = jnp.where(lanes < half + half // 2, ends, rest).astype(BF16)
    for at in range(3):
        sums[:, (4 + at) * pair : (5 + at) * pair] = tiles[at * pair : (at + 1) * pair].astype(BF16)


def sections_kernel(
    features, order, s0, s1, s2, s3, plain, f0, f1, f2, f3, out, stack, expand, made, sent
):
    pair = f0.shape[0]
    rank = pair // 2
    count, width = plain.shape
    cols = width // GROUPS
    for steps, ref in enumerate((f0, f1, f2, f3)):
        section = order[steps]
        expand[pl.ds(pl.multiple_of(section * rank, rank), rank), :] = ref[rank:]

    def summed(at):
        columns = slice(at * pair, (at + 1) * pair)
        parts = [ref[:, columns].astype(F32) for ref in (s0, s1, s2, s3)]
        return (parts[0] + parts[1]) + (parts[2] + parts[3])

    y = [summed(s) for s in range(4)]
    square = y[3][:, rank : rank + 1] + y[3][:, pair - 1 :]
    stacks = [summed(4 + at) for at in range(3)]

    def thirds(place):
        at = (place % 2) * rank
        value = stacks[place // 2][at : at + rank]
        high, rest = rounded(value)
        middle, rest = rounded(rest)
        return jnp.concatenate([high, middle, rest.astype(BF16)], axis=0)

    uses = (((1, 0), (2, 1), (3, 3)), ((2, 2), (3, 4)), ((3, 5),))
    lowers = []
    for s in range(4):
        scale = lax.rsqrt(jnp.maximum(square, 0.0) / features + 1e-05)
        lower = (y[s][:, :rank] * scale).astype(BF16)
        lowers.append(lower)
        if s == 3:
            break
        added = dot(
            jnp.concatenate([lower] * 3, axis=1),
            jnp.concatenate([thirds(place) for _, place in uses[s]], axis=1),
        )
        value = lower.astype(F32)
        for at, (later, _) in enumerate(uses[s]):
            y[later] = y[later] + added[:, at * pair : (at + 1) * pair]
        ends = added[:, added.shape[1] - rank :]
        square = square + jnp.sum(value * (2.0 * y[s][:, rank:] + ends), axis=1, keepdims=True)
    size = GROUPS * count
    moved = one_hot(block_places((1, size), 1, count), (size, size), 0)
    current = [plain[:, g * cols : (g + 1) * cols].astype(F32) for g in range(GROUPS)]
    sends = []
    for s in range(4):
        for g in range(GROUPS):
            columns = slice(g * cols, (g + 1) * cols)
            current[g] = current[g] + dot(lowers[s], expand[s * rank : (s + 1) * rank, columns])
            stack[s, g * count : (g + 1) * count] = current[g].astype(BF16)
        made[s] = dot(moved, stack[s]).astype(BF16)
        sends.append(
            pltpu.make_async_copy(made.at[s], out.at[pl.ds(s * size, size)], sent.at[s])
        )
        sends[-1].start()
    for copy in sends:
        copy.wait()


def unpack_kernel(places, back, out):
    size, cols = places.shape[0], back.shape[2]
    count = size // GROUPS
    chosen = one_hot(places[...], (size, back.shape[1]), 1)
    for plane in range(back.shape[0]):
        found = dot(chosen, back[plane]).astype(BF16)
        for g in range(GROUPS):
            start = (plane * GROUPS + g) * cols
            out[:, start : start + cols] = found[g * count : (g + 1) * count]


def local(hidden_in, request_adapter, home_slot, gains, shrink_tiles, expand_tiles):
    chips = lax.axis_size("chip")
    peers = 2 * chips
    sections = lax.axis_size("segment")
    plane = lax.axis_index("segment")
    core = lax.axis_index("core")
    count, width = hidden_in.shape
    part = width // sections
    cols = part // GROUPS
    total = home_slot.shape[0]
    rank = expand_tiles.shape[2]
    pair = 2 * rank
    depth = 2
    block = depth * GROUPS
    size = peers * block

    quarters = call(
        quarters_kernel,
        tuple(jax.ShapeDtypeStruct((pair, part), BF16) for _ in range(sections)),
        scratch=[
            pltpu.VMEM((sections, rank, part), BF16),
            pltpu.VMEM((1, width), F32),
            pltpu.SemaphoreType.DMA,
            pltpu.SemaphoreType.DMA((sections,)),
            pltpu.SemaphoreType.DMA((sections,)),
        ],
        specs=[SMEM, ANY, ANY, ANY],
        room=60,
        name="quarters",
    )(plane.reshape(1), shrink_tiles[0, 0].T, gains, expand_tiles[0, 0])

    adapter_ids = request_adapter[:, 0]
    catalog = jnp.arange(total, dtype=jnp.int32)
    storage = jnp.sum(
        jnp.where(adapter_ids[:, None] == catalog[None, :], home_slot[None, :], 0), axis=1
    )
    order = jnp.arange(count, dtype=jnp.int32)
    same_adapter = adapter_ids[:, None] == adapter_ids[None, :]
    earlier = jnp.sum((same_adapter & (order[None, :] < order[:, None])).astype(jnp.int32), axis=1)
    groups = jnp.arange(GROUPS, dtype=jnp.int32)[:, None] * depth
    homes = (groups + (storage * block + earlier)[None, :]).reshape(-1)

    mine = lax.dynamic_slice(hidden_in, (0, plane * part), (count, part))
    packed = call(
        pack_kernel,
        jax.ShapeDtypeStruct((size, cols), BF16),
        specs=[VMEM, VMEM],
        name="pack",
    )(homes[None, :], mine)
    held = [quarters[0]] + [
        shifted(quarters[steps], "segment", steps) for steps in range(1, sections)
    ]

    arrived = lax.all_to_all(
        packed.reshape(chips, 2 * block, cols), "chip", split_axis=0, concat_axis=0, tiled=True
    )

    section_order = (plane - jnp.arange(sections, dtype=jnp.int32)) % sections
    section_order = jnp.concatenate([section_order, core.reshape(1)])
    tiles = call(
        factors_kernel,
        jax.ShapeDtypeStruct((6 * rank, pair), F32),
        scratch=[
            pltpu.VMEM((sections * pair, part), BF16),
            pltpu.VMEM((sections * rank, part), BF16),
        ],
        specs=[SMEM] + [VMEM] * 4,
        flops=FACTOR_FLOPS,
        name="factors",
    )(section_order, *held)
    arrived, tiles = lax.optimization_barrier((arrived, tiles))

    theirs = lax.dynamic_slice(arrived, (0, (1 - core) * block, 0), (chips, block, cols))
    others = lax.ppermute(theirs, "core", [(0, 1), (1, 0)]).reshape(chips * block, cols)
    sums, plain = call(
        products_kernel,
        (
            jax.ShapeDtypeStruct((peers * depth, 7 * pair), BF16),
            jax.ShapeDtypeStruct((peers * depth, part), BF16),
        ),
        scratch=[pltpu.VMEM((peers * depth, sections * pair), F32)],
        specs=[SMEM] + [VMEM] * 7,
        name="products",
    )(section_order, arrived.reshape(size, cols), others, tiles, *held)
    all_sums = [sums] + [shifted(sums, "segment", steps) for steps in range(1, sections)]

    results = call(
        lambda *refs: sections_kernel(width, *refs),
        jax.ShapeDtypeStruct((sections * size, cols), BF16),
        scratch=[
            pltpu.VMEM((sections, size, cols), BF16),
            pltpu.VMEM((sections * rank, part), BF16),
            pltpu.VMEM((sections, size, cols), BF16),
            pltpu.SemaphoreType.DMA((sections,)),
        ],
        specs=[SMEM] + [VMEM] * 9,
        out_spec=ANY,
        name="sections",
    )(section_order, *all_sums, plain, *held)

    back = lax.all_to_all(
        results.reshape(sections * peers, block, cols),
        ("segment", "chip", "core"),
        split_axis=0,
        concat_axis=0,
        tiled=True,
    )
    rows = call(
        unpack_kernel,
        jax.ShapeDtypeStruct((count, width), BF16),
        specs=[VMEM, VMEM],
        name="unpack",
    )(homes[:, None], back.reshape(sections, size, cols))
    return rows[None]


def solution(mesh):
    planes, peers = mesh.devices.shape
    split = Mesh(mesh.devices.reshape(planes, peers // 2, 2), ("segment", "chip", "core"))
    rows = ("chip", "core")
    return jax.shard_map(
        local,
        mesh=split,
        in_specs=(
            P(rows, None),
            P(rows, None),
            P(),
            P("segment", None),
            P("segment", rows, None, None),
            P("segment", rows, None, None),
        ),
        out_specs=P("segment", rows, None),
        check_vma=False,
    )
```

```python
import jax
import jax.numpy as jnp
from jax import lax
from jax.experimental import pallas as pl
from jax.experimental.pallas import tpu as pltpu
from jax.sharding import Mesh
from jax.sharding import PartitionSpec as P

GROUPS = 4
FACTOR_FLOPS = 40_000_000_000
VMEM = pl.BlockSpec(memory_space=pltpu.VMEM)
ANY = pl.BlockSpec(memory_space=pl.ANY)
SMEM = pl.BlockSpec(memory_space=pltpu.SMEM)
F32 = jnp.float32
BF16 = jnp.bfloat16


def shifted(value, axis, steps):
    count = lax.axis_size(axis)
    return lax.ppermute(value, axis, [(source, (source + steps) % count) for source in range(count)])


def dot(a, b, contract_b=0, precision=None):
    return lax.dot_general(
        a, b, (((1,), (contract_b,)), ((), ())), precision=precision, preferred_element_type=F32
    )


def call(kernel, outs, *, scratch=(), flops=0, specs=None, out_spec=VMEM, room=48, **options):
    return pl.pallas_call(
        kernel,
        out_shape=outs,
        in_specs=specs,
        out_specs=jax.tree.map(lambda _: out_spec, outs),
        scratch_shapes=list(scratch),
        compiler_params=pltpu.CompilerParams(vmem_limit_bytes=room * 1024 * 1024),
        cost_estimate=pl.CostEstimate(flops=flops, bytes_accessed=4 << 20, transcendentals=0),
        **options,
    )


def one_hot(places, shape, axis):
    lines = lax.broadcasted_iota(jnp.int32, shape, axis)
    return jnp.where(lines == places, 1.0, 0.0).astype(BF16)


def block_places(shape, axis, count, core=None, only=None):
    line = lax.broadcasted_iota(jnp.int32, shape, axis)
    group = line // count
    row = line % count
    within = group * 2 + row % 2
    peer = row // 2
    if core is None:
        return peer * (2 * GROUPS) + within
    if only:
        return jnp.where(peer % 2 == core, peer * (2 * GROUPS) + within, -1)
    return jnp.where(peer % 2 == core, -1, (peer // 2) * (2 * GROUPS) + within)


def quarter_columns(plane, steps, part, planes=4):
    return pl.ds(pl.multiple_of(lax.rem(plane + steps, planes) * part, part), part)


def pack_kernel(places, hidden, out):
    cols = out.shape[1]
    chosen = one_hot(places[...], (out.shape[0], places.shape[1]), 0)
    stacked = jnp.concatenate(
        [hidden[:, g * cols : (g + 1) * cols] for g in range(GROUPS)], axis=0
    )
    out[...] = dot(chosen, stacked).astype(BF16)


def quarters_kernel(
    plane, shrink, gain, expand, q0, q1, q2, q3, made, weights, gain_in, in_sem, put_sem, out_sem
):
    rank = shrink.shape[0]
    outs = (q0, q1, q2, q3)
    part = q0.shape[1]
    columns = [
        pl.ds(pl.multiple_of(lax.rem(plane[0] + k, 4) * part, part), part) for k in range(4)
    ]
    load = pltpu.make_async_copy(gain, weights, gain_in)
    load.start()
    order = (2, 1, 3, 0)
    ins, puts, sends = {}, {}, {}
    for k in order:
        ins[k] = pltpu.make_async_copy(
            shrink.at[:, columns[k]], made.at[k, pl.ds(0, rank)], in_sem.at[k]
        )
        puts[k] = pltpu.make_async_copy(
            expand.at[:, columns[k]], made.at[k, pl.ds(rank, rank)], put_sem.at[k]
        )
        ins[k].start()
        puts[k].start()
    load.wait()
    for k in order:
        ins[k].wait()
        made[k, :rank] = (made[k, :rank].astype(F32) * weights[:, columns[k]]).astype(BF16)
        puts[k].wait()
        sends[k] = pltpu.make_async_copy(made.at[k], outs[k], out_sem.at[k])
        sends[k].start()
    for k in order:
        sends[k].wait()


def factors_kernel(order, own, first, second, third, tiles, every, expand):
    pair = own.shape[0]
    rank = pair // 2
    for steps, ref in enumerate((own, first, second, third)):
        section = order[steps]
        every[pl.ds(pl.multiple_of(section * pair, pair), pair), :] = ref[...]
        expand[pl.ds(pl.multiple_of(section * rank, rank), rank), :] = ref[rank:]
    product = dot(expand[: 3 * rank], every[...], 1)

    def tile(row, section):
        return product[row * rank : (row + 1) * rank, section * pair : (section + 1) * pair]

    lanes = lax.broadcasted_iota(jnp.int32, (rank, pair), 1)

    def last(row):
        return jnp.where(lanes < rank, tile(row, 3), tile(row, row))

    for place, value in enumerate(
        (tile(0, 1), tile(0, 2), tile(1, 2), last(0), last(1), last(2))
    ):
        tiles[place * rank : (place + 1) * rank] = value


def rounded(value):
    high = value.astype(BF16)
    return high, value - high.astype(F32)


def products_kernel(
    order, blocks, others, tiles, own, first, second, third, sums, plain, product
):
    count, width = plain.shape
    cols = width // GROUPS
    size = count * GROUPS
    core = order[4]
    stacked = dot(
        one_hot(block_places((size, 1), 0, count, core, True), (size, blocks.shape[0]), 1),
        blocks[...],
    ) + dot(
        one_hot(block_places((size, 1), 0, count, core, False), (size, others.shape[0]), 1),
        others[...],
    )
    stacked = stacked.astype(BF16)
    for g in range(GROUPS):
        plain[:, g * cols : (g + 1) * cols] = stacked[g * count : (g + 1) * count]
    rows = plain[...]
    pair = own.shape[0]
    half = pair // 2
    for steps, ref in enumerate((own, first, second, third)):
        section = order[steps]
        product[:, pl.ds(pl.multiple_of(section * pair, pair), pair)] = dot(rows, ref[...], 1)
    values = rows.astype(F32)
    squares = jnp.sum(values * values, axis=1, keepdims=True)
    lanes = lax.broadcasted_iota(jnp.int32, (count, pair), 1)
    sums[:, : 3 * pair] = product[:, : 3 * pair].astype(BF16)
    high, rest = rounded(squares)
    ends = jnp.where(lanes < half, product[:, 3 * pair :], high.astype(F32))
    sums[:, 3 * pair : 4 * pair] = jnp.where(lanes < half + half // 2, ends, rest).astype(BF16)
    for at in range(3):
        sums[:, (4 + at) * pair : (5 + at) * pair] = tiles[at * pair : (at + 1) * pair].astype(BF16)


def sections_kernel(
    features, order, s0, s1, s2, s3, plain, f0, f1, f2, f3, out, stack, expand, made, sent
):
    pair = f0.shape[0]
    rank = pair // 2
    count, width = plain.shape
    cols = width // GROUPS
    for steps, ref in enumerate((f0, f1, f2, f3)):
        section = order[steps]
        expand[pl.ds(pl.multiple_of(section * rank, rank), rank), :] = ref[rank:]

    def summed(at):
        columns = slice(at * pair, (at + 1) * pair)
        parts = [ref[:, columns].astype(F32) for ref in (s0, s1, s2, s3)]
        return (parts[0] + parts[1]) + (parts[2] + parts[3])

    y = [summed(s) for s in range(4)]
    square = y[3][:, rank : rank + 1] + y[3][:, pair - 1 :]
    stacks = [summed(4 + at) for at in range(3)]

    def thirds(place):
        at = (place % 2) * rank
        value = stacks[place // 2][at : at + rank]
        high, rest = rounded(value)
        middle, rest = rounded(rest)
        return jnp.concatenate([high, middle, rest.astype(BF16)], axis=0)

    uses = (((1, 0), (2, 1), (3, 3)), ((2, 2), (3, 4)), ((3, 5),))
    size = GROUPS * count
    moved = one_hot(block_places((1, size), 1, count), (size, size), 0)
    current = [plain[:, g * cols : (g + 1) * cols].astype(F32) for g in range(GROUPS)]
    sends = []
    for s in range(4):
        scale = lax.rsqrt(jnp.maximum(square, 0.0) / features + 1e-05)
        lower = (y[s][:, :rank] * scale).astype(BF16)
        if s < 3:
            added = dot(
                jnp.concatenate([lower] * 3, axis=1),
                jnp.concatenate([thirds(place) for _, place in uses[s]], axis=1),
            )
            value = lower.astype(F32)
            for at, (later, _) in enumerate(uses[s]):
                y[later] = y[later] + added[:, at * pair : (at + 1) * pair]
            ends = added[:, added.shape[1] - rank :]
            square = square + jnp.sum(
                value * (2.0 * y[s][:, rank:] + ends), axis=1, keepdims=True
            )
        for g in range(GROUPS):
            columns = slice(g * cols, (g + 1) * cols)
            current[g] = current[g] + dot(lower, expand[s * rank : (s + 1) * rank, columns])
            stack[s, g * count : (g + 1) * count] = current[g].astype(BF16)
        made[s] = dot(moved, stack[s]).astype(BF16)
        sends.append(
            pltpu.make_async_copy(made.at[s], out.at[pl.ds(s * size, size)], sent.at[s])
        )
        sends[-1].start()
    for copy in sends:
        copy.wait()


def unpack_kernel(places, back, out, made, sent):
    size, cols = places.shape[0], back.shape[2]
    count = size // GROUPS
    part = GROUPS * cols
    chosen = one_hot(places[...], (size, back.shape[1]), 1)
    sends = []
    for plane in range(back.shape[0]):
        found = dot(chosen, back[plane]).astype(BF16)
        for g in range(GROUPS):
            made[plane, :, g * cols : (g + 1) * cols] = found[g * count : (g + 1) * count]
        sends.append(
            pltpu.make_async_copy(
                made.at[plane], out.at[:, pl.ds(plane * part, part)], sent.at[plane]
            )
        )
        sends[-1].start()
    for copy in sends:
        copy.wait()


def local(hidden_in, request_adapter, home_slot, gains, shrink_tiles, expand_tiles):
    chips = lax.axis_size("chip")
    peers = 2 * chips
    sections = lax.axis_size("segment")
    plane = lax.axis_index("segment")
    core = lax.axis_index("core")
    count, width = hidden_in.shape
    part = width // sections
    cols = part // GROUPS
    total = home_slot.shape[0]
    rank = expand_tiles.shape[2]
    pair = 2 * rank
    depth = 2
    block = depth * GROUPS
    size = peers * block

    quarters = call(
        quarters_kernel,
        tuple(jax.ShapeDtypeStruct((pair, part), BF16) for _ in range(sections)),
        scratch=[
            pltpu.VMEM((sections, pair, part), BF16),
            pltpu.VMEM((1, width), F32),
            pltpu.SemaphoreType.DMA,
            pltpu.SemaphoreType.DMA((sections,)),
            pltpu.SemaphoreType.DMA((sections,)),
            pltpu.SemaphoreType.DMA((sections,)),
        ],
        out_spec=ANY,
        specs=[SMEM, ANY, ANY, ANY],
        room=60,
        name="quarters",
    )(plane.reshape(1), shrink_tiles[0, 0].T, gains, expand_tiles[0, 0])

    adapter_ids = request_adapter[:, 0]
    catalog = jnp.arange(total, dtype=jnp.int32)
    storage = jnp.sum(
        jnp.where(adapter_ids[:, None] == catalog[None, :], home_slot[None, :], 0), axis=1
    )
    order = jnp.arange(count, dtype=jnp.int32)
    same_adapter = adapter_ids[:, None] == adapter_ids[None, :]
    earlier = jnp.sum((same_adapter & (order[None, :] < order[:, None])).astype(jnp.int32), axis=1)
    groups = jnp.arange(GROUPS, dtype=jnp.int32)[:, None] * depth
    homes = (groups + (storage * block + earlier)[None, :]).reshape(-1)

    mine = lax.dynamic_slice(hidden_in, (0, plane * part), (count, part))
    packed = call(
        pack_kernel,
        jax.ShapeDtypeStruct((size, cols), BF16),
        specs=[VMEM, VMEM],
        name="pack",
    )(homes[None, :], mine)
    held = [quarters[0]] + [
        shifted(quarters[steps], "segment", steps) for steps in range(1, sections)
    ]

    arrived = lax.all_to_all(
        packed.reshape(chips, 2 * block, cols), "chip", split_axis=0, concat_axis=0, tiled=True
    )

    section_order = (plane - jnp.arange(sections, dtype=jnp.int32)) % sections
    section_order = jnp.concatenate([section_order, core.reshape(1)])
    tiles = call(
        factors_kernel,
        jax.ShapeDtypeStruct((6 * rank, pair), F32),
        scratch=[
            pltpu.VMEM((sections * pair, part), BF16),
            pltpu.VMEM((sections * rank, part), BF16),
        ],
        specs=[SMEM] + [VMEM] * 4,
        flops=FACTOR_FLOPS,
        name="factors",
    )(section_order, *held)
    arrived, tiles = lax.optimization_barrier((arrived, tiles))

    theirs = lax.dynamic_slice(arrived, (0, (1 - core) * block, 0), (chips, block, cols))
    others = lax.ppermute(theirs, "core", [(0, 1), (1, 0)]).reshape(chips * block, cols)
    sums, plain = call(
        products_kernel,
        (
            jax.ShapeDtypeStruct((peers * depth, 7 * pair), BF16),
            jax.ShapeDtypeStruct((peers * depth, part), BF16),
        ),
        scratch=[pltpu.VMEM((peers * depth, sections * pair), F32)],
        specs=[SMEM] + [VMEM] * 7,
        name="products",
    )(section_order, arrived.reshape(size, cols), others, tiles, *held)
    all_sums = [sums] + [shifted(sums, "segment", steps) for steps in range(1, sections)]

    results = call(
        lambda *refs: sections_kernel(width, *refs),
        jax.ShapeDtypeStruct((sections * size, cols), BF16),
        scratch=[
            pltpu.VMEM((sections, size, cols), BF16),
            pltpu.VMEM((sections * rank, part), BF16),
            pltpu.VMEM((sections, size, cols), BF16),
            pltpu.SemaphoreType.DMA((sections,)),
        ],
        specs=[SMEM] + [VMEM] * 9,
        out_spec=ANY,
        name="sections",
    )(section_order, *all_sums, plain, *held)

    back = lax.all_to_all(
        results.reshape(sections * peers, block, cols),
        ("segment", "chip", "core"),
        split_axis=0,
        concat_axis=0,
        tiled=True,
    )
    rows = call(
        unpack_kernel,
        jax.ShapeDtypeStruct((count, width), BF16),
        scratch=[
            pltpu.VMEM((sections, count, part), BF16),
            pltpu.SemaphoreType.DMA((sections,)),
        ],
        specs=[VMEM, VMEM],
        out_spec=ANY,
        name="unpack",
    )(homes[:, None], back.reshape(sections, size, cols))
    return rows[None]


def solution(mesh):
    planes, peers = mesh.devices.shape
    split = Mesh(mesh.devices.reshape(planes, peers // 2, 2), ("segment", "chip", "core"))
    rows = ("chip", "core")
    return jax.shard_map(
        local,
        mesh=split,
        in_specs=(
            P(rows, None),
            P(rows, None),
            P(),
            P("segment", None),
            P("segment", rows, None, None),
            P("segment", rows, None, None),
        ),
        out_specs=P("segment", rows, None),
        check_vma=False,
    )
```

```python
import jax
import jax.numpy as jnp
from jax import lax
from jax.experimental import pallas as pl
from jax.experimental.pallas import tpu as pltpu
from jax.sharding import Mesh
from jax.sharding import PartitionSpec as P

GROUPS = 4
LANDED_FLOPS = 40_000_000_000
VMEM = pl.BlockSpec(memory_space=pltpu.VMEM)
ANY = pl.BlockSpec(memory_space=pl.ANY)
SMEM = pl.BlockSpec(memory_space=pltpu.SMEM)
F32 = jnp.float32
BF16 = jnp.bfloat16


def shifted(value, axis, steps):
    count = lax.axis_size(axis)
    return lax.ppermute(value, axis, [(source, (source + steps) % count) for source in range(count)])


def dot(a, b, contract_b=0, precision=None):
    return lax.dot_general(
        a, b, (((1,), (contract_b,)), ((), ())), precision=precision, preferred_element_type=F32
    )


def call(kernel, outs, *, scratch=(), flops=0, specs=None, out_spec=VMEM, room=48, **options):
    return pl.pallas_call(
        kernel,
        out_shape=outs,
        in_specs=specs,
        out_specs=jax.tree.map(lambda _: out_spec, outs),
        scratch_shapes=list(scratch),
        compiler_params=pltpu.CompilerParams(vmem_limit_bytes=room * 1024 * 1024),
        cost_estimate=pl.CostEstimate(flops=flops, bytes_accessed=4 << 20, transcendentals=0),
        **options,
    )


def one_hot(places, shape, axis):
    lines = lax.broadcasted_iota(jnp.int32, shape, axis)
    return jnp.where(lines == places, 1.0, 0.0).astype(BF16)


def block_places(shape, axis, count, core=None, only=None):
    line = lax.broadcasted_iota(jnp.int32, shape, axis)
    group = line // count
    row = line % count
    within = group * 2 + row % 2
    peer = row // 2
    if core is None:
        return peer * (2 * GROUPS) + within
    if only:
        return jnp.where(peer % 2 == core, peer * (2 * GROUPS) + within, -1)
    return jnp.where(peer % 2 == core, -1, (peer // 2) * (2 * GROUPS) + within)


def quarter_columns(plane, steps, part, planes=4):
    return pl.ds(pl.multiple_of(lax.rem(plane + steps, planes) * part, part), part)


def pack_kernel(places, hidden, out):
    cols = out.shape[1]
    chosen = one_hot(places[...], (out.shape[0], places.shape[1]), 0)
    stacked = jnp.concatenate(
        [hidden[:, g * cols : (g + 1) * cols] for g in range(GROUPS)], axis=0
    )
    out[...] = dot(chosen, stacked).astype(BF16)


def quarters_kernel(
    plane, shrink, gain, expand, q0, q1, q2, q3, made, weights, gain_in, in_sem, put_sem, out_sem
):
    rank = shrink.shape[0]
    outs = (q0, q1, q2, q3)
    part = q0.shape[1]
    columns = [
        pl.ds(pl.multiple_of(lax.rem(plane[0] + k, 4) * part, part), part) for k in range(4)
    ]
    load = pltpu.make_async_copy(gain, weights, gain_in)
    load.start()
    order = (2, 1, 3, 0)
    ins, puts, sends = {}, {}, {}
    for k in order:
        ins[k] = pltpu.make_async_copy(
            shrink.at[:, columns[k]], made.at[k, pl.ds(0, rank)], in_sem.at[k]
        )
        puts[k] = pltpu.make_async_copy(
            expand.at[:, columns[k]], made.at[k, pl.ds(rank, rank)], put_sem.at[k]
        )
        ins[k].start()
        puts[k].start()
    load.wait()
    for k in order:
        ins[k].wait()
        made[k, :rank] = (made[k, :rank].astype(F32) * weights[:, columns[k]]).astype(BF16)
        puts[k].wait()
        sends[k] = pltpu.make_async_copy(made.at[k], outs[k], out_sem.at[k])
        sends[k].start()
    for k in order:
        sends[k].wait()


def factors_kernel(order, own, first, second, third, tiles, every, expand):
    pair = own.shape[0]
    rank = pair // 2
    for steps, ref in enumerate((own, first, second, third)):
        section = order[steps]
        every[pl.ds(pl.multiple_of(section * pair, pair), pair), :] = ref[...]
        expand[pl.ds(pl.multiple_of(section * rank, rank), rank), :] = ref[rank:]
    product = dot(expand[: 3 * rank], every[...], 1)

    def tile(row, section):
        return product[row * rank : (row + 1) * rank, section * pair : (section + 1) * pair]

    lanes = lax.broadcasted_iota(jnp.int32, (rank, pair), 1)

    def last(row):
        return jnp.where(lanes < rank, tile(row, 3), tile(row, row))

    for place, value in enumerate(
        (tile(0, 1), tile(0, 2), tile(1, 2), last(0), last(1), last(2))
    ):
        tiles[place * rank : (place + 1) * rank] = value


def rounded(value):
    high = value.astype(BF16)
    return high, value - high.astype(F32)


def landed_kernel(first, second, third, token):
    del first, second, third
    token[...] = jnp.zeros_like(token)


def products_kernel(
    order, token, blocks, others, tiles, own, first, second, third, sums, plain, product
):
    count, width = plain.shape
    cols = width // GROUPS
    size = count * GROUPS
    core = order[4]
    del token
    stacked = dot(
        one_hot(block_places((size, 1), 0, count, core, True), (size, blocks.shape[0]), 1),
        blocks[...],
    ) + dot(
        one_hot(block_places((size, 1), 0, count, core, False), (size, others.shape[0]), 1),
        others[...],
    )
    stacked = stacked.astype(BF16)
    for g in range(GROUPS):
        plain[:, g * cols : (g + 1) * cols] = stacked[g * count : (g + 1) * count]
    rows = plain[...]
    pair = own.shape[0]
    half = pair // 2
    for steps, ref in enumerate((own, first, second, third)):
        section = order[steps]
        product[:, pl.ds(pl.multiple_of(section * pair, pair), pair)] = dot(rows, ref[...], 1)
    values = rows.astype(F32)
    squares = jnp.sum(values * values, axis=1, keepdims=True)
    lanes = lax.broadcasted_iota(jnp.int32, (count, pair), 1)
    sums[:, : 3 * pair] = product[:, : 3 * pair].astype(BF16)
    high, rest = rounded(squares)
    ends = jnp.where(lanes < half, product[:, 3 * pair :], high.astype(F32))
    sums[:, 3 * pair : 4 * pair] = jnp.where(lanes < half + half // 2, ends, rest).astype(BF16)
    for at in range(3):
        sums[:, (4 + at) * pair : (5 + at) * pair] = tiles[at * pair : (at + 1) * pair].astype(BF16)


def sections_kernel(
    features, order, s0, s1, s2, s3, plain, f0, f1, f2, f3, out, stack, expand, made, sent
):
    pair = f0.shape[0]
    rank = pair // 2
    count, width = plain.shape
    cols = width // GROUPS
    for steps, ref in enumerate((f0, f1, f2, f3)):
        section = order[steps]
        expand[pl.ds(pl.multiple_of(section * rank, rank), rank), :] = ref[rank:]

    def summed(at):
        columns = slice(at * pair, (at + 1) * pair)
        parts = [ref[:, columns].astype(F32) for ref in (s0, s1, s2, s3)]
        return (parts[0] + parts[1]) + (parts[2] + parts[3])

    y = [summed(s) for s in range(4)]
    square = y[3][:, rank : rank + 1] + y[3][:, pair - 1 :]
    stacks = [summed(4 + at) for at in range(3)]

    def thirds(place):
        at = (place % 2) * rank
        value = stacks[place // 2][at : at + rank]
        high, rest = rounded(value)
        middle, rest = rounded(rest)
        return jnp.concatenate([high, middle, rest.astype(BF16)], axis=0)

    uses = (((1, 0), (2, 1), (3, 3)), ((2, 2), (3, 4)), ((3, 5),))
    size = GROUPS * count
    moved = one_hot(block_places((1, size), 1, count), (size, size), 0)
    current = [plain[:, g * cols : (g + 1) * cols].astype(F32) for g in range(GROUPS)]
    sends = []
    for s in range(4):
        scale = lax.rsqrt(jnp.maximum(square, 0.0) / features + 1e-05)
        lower = (y[s][:, :rank] * scale).astype(BF16)
        if s < 3:
            added = dot(
                jnp.concatenate([lower] * 3, axis=1),
                jnp.concatenate([thirds(place) for _, place in uses[s]], axis=1),
            )
            value = lower.astype(F32)
            for at, (later, _) in enumerate(uses[s]):
                y[later] = y[later] + added[:, at * pair : (at + 1) * pair]
            ends = added[:, added.shape[1] - rank :]
            square = square + jnp.sum(
                value * (2.0 * y[s][:, rank:] + ends), axis=1, keepdims=True
            )
        for g in range(GROUPS):
            columns = slice(g * cols, (g + 1) * cols)
            current[g] = current[g] + dot(lower, expand[s * rank : (s + 1) * rank, columns])
            stack[s, g * count : (g + 1) * count] = current[g].astype(BF16)
        made[s] = dot(moved, stack[s]).astype(BF16)
        sends.append(
            pltpu.make_async_copy(made.at[s], out.at[pl.ds(s * size, size)], sent.at[s])
        )
        sends[-1].start()
    for copy in sends:
        copy.wait()


def unpack_kernel(places, back, out, made, sent):
    size, cols = places.shape[0], back.shape[2]
    count = size // GROUPS
    part = GROUPS * cols
    chosen = one_hot(places[...], (size, back.shape[1]), 1)
    sends = []
    for plane in range(back.shape[0]):
        found = dot(chosen, back[plane]).astype(BF16)
        for g in range(GROUPS):
            made[plane, :, g * cols : (g + 1) * cols] = found[g * count : (g + 1) * count]
        sends.append(
            pltpu.make_async_copy(
                made.at[plane], out.at[:, pl.ds(plane * part, part)], sent.at[plane]
            )
        )
        sends[-1].start()
    for copy in sends:
        copy.wait()


def local(hidden_in, request_adapter, home_slot, gains, shrink_tiles, expand_tiles):
    chips = lax.axis_size("chip")
    peers = 2 * chips
    sections = lax.axis_size("segment")
    plane = lax.axis_index("segment")
    core = lax.axis_index("core")
    count, width = hidden_in.shape
    part = width // sections
    cols = part // GROUPS
    total = home_slot.shape[0]
    rank = expand_tiles.shape[2]
    pair = 2 * rank
    depth = 2
    block = depth * GROUPS
    size = peers * block

    quarters = call(
        quarters_kernel,
        tuple(jax.ShapeDtypeStruct((pair, part), BF16) for _ in range(sections)),
        scratch=[
            pltpu.VMEM((sections, pair, part), BF16),
            pltpu.VMEM((1, width), F32),
            pltpu.SemaphoreType.DMA,
            pltpu.SemaphoreType.DMA((sections,)),
            pltpu.SemaphoreType.DMA((sections,)),
            pltpu.SemaphoreType.DMA((sections,)),
        ],
        out_spec=ANY,
        specs=[SMEM, ANY, ANY, ANY],
        room=60,
        name="quarters",
    )(plane.reshape(1), shrink_tiles[0, 0].T, gains, expand_tiles[0, 0])

    adapter_ids = request_adapter[:, 0]
    catalog = jnp.arange(total, dtype=jnp.int32)
    storage = jnp.sum(
        jnp.where(adapter_ids[:, None] == catalog[None, :], home_slot[None, :], 0), axis=1
    )
    order = jnp.arange(count, dtype=jnp.int32)
    same_adapter = adapter_ids[:, None] == adapter_ids[None, :]
    earlier = jnp.sum((same_adapter & (order[None, :] < order[:, None])).astype(jnp.int32), axis=1)
    groups = jnp.arange(GROUPS, dtype=jnp.int32)[:, None] * depth
    homes = (groups + (storage * block + earlier)[None, :]).reshape(-1)

    mine = lax.dynamic_slice(hidden_in, (0, plane * part), (count, part))
    packed = call(
        pack_kernel,
        jax.ShapeDtypeStruct((size, cols), BF16),
        specs=[VMEM, VMEM],
        name="pack",
    )(homes[None, :], mine)
    held = [quarters[0]] + [
        shifted(quarters[steps], "segment", steps) for steps in range(1, sections)
    ]

    arrived = lax.all_to_all(
        packed.reshape(chips, 2 * block, cols), "chip", split_axis=0, concat_axis=0, tiled=True
    )

    section_order = (plane - jnp.arange(sections, dtype=jnp.int32)) % sections
    section_order = jnp.concatenate([section_order, core.reshape(1)])
    tiles = call(
        factors_kernel,
        jax.ShapeDtypeStruct((6 * rank, pair), F32),
        scratch=[
            pltpu.VMEM((sections * pair, part), BF16),
            pltpu.VMEM((sections * rank, part), BF16),
        ],
        specs=[SMEM] + [VMEM] * 4,
        name="factors",
    )(section_order, *held)
    token = call(
        landed_kernel,
        jax.ShapeDtypeStruct((8, 128), F32),
        specs=[ANY] * 3,
        flops=LANDED_FLOPS,
        name="landed",
    )(*held[1:])
    arrived, token = lax.optimization_barrier((arrived, token))

    theirs = lax.dynamic_slice(arrived, (0, (1 - core) * block, 0), (chips, block, cols))
    others = lax.ppermute(theirs, "core", [(0, 1), (1, 0)]).reshape(chips * block, cols)
    sums, plain = call(
        products_kernel,
        (
            jax.ShapeDtypeStruct((peers * depth, 7 * pair), BF16),
            jax.ShapeDtypeStruct((peers * depth, part), BF16),
        ),
        scratch=[pltpu.VMEM((peers * depth, sections * pair), F32)],
        specs=[SMEM, ANY] + [VMEM] * 7,
        name="products",
    )(section_order, token, arrived.reshape(size, cols), others, tiles, *held)
    all_sums = [sums] + [shifted(sums, "segment", steps) for steps in range(1, sections)]

    results = call(
        lambda *refs: sections_kernel(width, *refs),
        jax.ShapeDtypeStruct((sections * size, cols), BF16),
        scratch=[
            pltpu.VMEM((sections, size, cols), BF16),
            pltpu.VMEM((sections * rank, part), BF16),
            pltpu.VMEM((sections, size, cols), BF16),
            pltpu.SemaphoreType.DMA((sections,)),
        ],
        specs=[SMEM] + [VMEM] * 9,
        out_spec=ANY,
        name="sections",
    )(section_order, *all_sums, plain, *held)

    back = lax.all_to_all(
        results.reshape(sections * peers, block, cols),
        ("segment", "chip", "core"),
        split_axis=0,
        concat_axis=0,
        tiled=True,
    )
    rows = call(
        unpack_kernel,
        jax.ShapeDtypeStruct((count, width), BF16),
        scratch=[
            pltpu.VMEM((sections, count, part), BF16),
            pltpu.SemaphoreType.DMA((sections,)),
        ],
        specs=[VMEM, VMEM],
        out_spec=ANY,
        name="unpack",
    )(homes[:, None], back.reshape(sections, size, cols))
    return rows[None]


def solution(mesh):
    planes, peers = mesh.devices.shape
    split = Mesh(mesh.devices.reshape(planes, peers // 2, 2), ("segment", "chip", "core"))
    rows = ("chip", "core")
    return jax.shard_map(
        local,
        mesh=split,
        in_specs=(
            P(rows, None),
            P(rows, None),
            P(),
            P("segment", None),
            P("segment", rows, None, None),
            P("segment", rows, None, None),
        ),
        out_specs=P("segment", rows, None),
        check_vma=False,
    )
```

```python
import jax
import jax.numpy as jnp
from jax import lax
from jax.experimental import pallas as pl
from jax.experimental.pallas import tpu as pltpu
from jax.sharding import Mesh
from jax.sharding import PartitionSpec as P

GROUPS = 4
LANDED_FLOPS = 40_000_000_000
VMEM = pl.BlockSpec(memory_space=pltpu.VMEM)
ANY = pl.BlockSpec(memory_space=pl.ANY)
SMEM = pl.BlockSpec(memory_space=pltpu.SMEM)
F32 = jnp.float32
BF16 = jnp.bfloat16


def shifted(value, axis, steps):
    count = lax.axis_size(axis)
    return lax.ppermute(value, axis, [(source, (source + steps) % count) for source in range(count)])


def dot(a, b, contract_b=0, precision=None):
    return lax.dot_general(
        a, b, (((1,), (contract_b,)), ((), ())), precision=precision, preferred_element_type=F32
    )


def call(kernel, outs, *, scratch=(), flops=0, specs=None, out_spec=VMEM, room=48, **options):
    return pl.pallas_call(
        kernel,
        out_shape=outs,
        in_specs=specs,
        out_specs=jax.tree.map(lambda _: out_spec, outs),
        scratch_shapes=list(scratch),
        compiler_params=pltpu.CompilerParams(vmem_limit_bytes=room * 1024 * 1024),
        cost_estimate=pl.CostEstimate(flops=flops, bytes_accessed=4 << 20, transcendentals=0),
        **options,
    )


def one_hot(places, shape, axis):
    lines = lax.broadcasted_iota(jnp.int32, shape, axis)
    return jnp.where(lines == places, 1.0, 0.0).astype(BF16)


def block_places(shape, axis, count, core=None, own=None):
    line = lax.broadcasted_iota(jnp.int32, shape, axis)
    group = line // count
    row = line % count
    within = group * 2 + row % 2
    peer = row // 2
    if core is None:
        return peer * (2 * GROUPS) + within
    held = peer % 2 == (core if own else 1 - core)
    return jnp.where(held, (peer - peer % 2 + core) * (2 * GROUPS) + within, -1)


def pack_kernel(places, hidden, out):
    cols = out.shape[1]
    chosen = one_hot(places[...], (out.shape[0], places.shape[1]), 0)
    stacked = jnp.concatenate(
        [hidden[:, g * cols : (g + 1) * cols] for g in range(GROUPS)], axis=0
    )
    out[...] = dot(chosen, stacked).astype(BF16)


def quarters_kernel(
    plane, shrink, gain, expand, q0, q1, q2, q3, made, weights, gain_in, in_sem, put_sem, out_sem
):
    rank = shrink.shape[0]
    outs = (q0, q1, q2, q3)
    part = q0.shape[1]
    columns = [
        pl.ds(pl.multiple_of(lax.rem(plane[0] + k, 4) * part, part), part) for k in range(4)
    ]
    load = pltpu.make_async_copy(gain, weights, gain_in)
    load.start()
    order = (2, 1, 3, 0)
    ins, puts, sends = {}, {}, {}
    for k in order:
        ins[k] = pltpu.make_async_copy(
            shrink.at[:, columns[k]], made.at[k, pl.ds(0, rank)], in_sem.at[k]
        )
        puts[k] = pltpu.make_async_copy(
            expand.at[:, columns[k]], made.at[k, pl.ds(rank, rank)], put_sem.at[k]
        )
        ins[k].start()
        puts[k].start()
    load.wait()
    for k in order:
        ins[k].wait()
        made[k, :rank] = (made[k, :rank].astype(F32) * weights[:, columns[k]]).astype(BF16)
        puts[k].wait()
        sends[k] = pltpu.make_async_copy(made.at[k], outs[k], out_sem.at[k])
        sends[k].start()
    for k in order:
        sends[k].wait()


def factors_kernel(order, own, first, second, third, tiles, every, expand):
    pair = own.shape[0]
    rank = pair // 2
    for steps, ref in enumerate((own, first, second, third)):
        section = order[steps]
        every[pl.ds(pl.multiple_of(section * pair, pair), pair), :] = ref[...]
        expand[pl.ds(pl.multiple_of(section * rank, rank), rank), :] = ref[rank:]
    product = dot(expand[: 3 * rank], every[...], 1)

    def tile(row, section):
        return product[row * rank : (row + 1) * rank, section * pair : (section + 1) * pair]

    lanes = lax.broadcasted_iota(jnp.int32, (rank, pair), 1)

    def last(row):
        return jnp.where(lanes < rank, tile(row, 3), tile(row, row))

    for place, value in enumerate(
        (tile(0, 1), tile(0, 2), tile(1, 2), last(0), last(1), last(2))
    ):
        tiles[place * rank : (place + 1) * rank] = value


def rounded(value):
    high = value.astype(BF16)
    return high, value - high.astype(F32)


def landed_kernel(first, second, third, token):
    del first, second, third
    token[...] = jnp.zeros_like(token)


def products_kernel(
    order, token, blocks, others, tiles, own, first, second, third, sums, plain, product
):
    count, width = plain.shape
    cols = width // GROUPS
    size = count * GROUPS
    core = order[4]
    del token
    stacked = dot(
        one_hot(block_places((size, 1), 0, count, core, True), (size, blocks.shape[0]), 1),
        blocks[...],
    ) + dot(
        one_hot(block_places((size, 1), 0, count, core, False), (size, others.shape[0]), 1),
        others[...],
    )
    stacked = stacked.astype(BF16)
    for g in range(GROUPS):
        plain[:, g * cols : (g + 1) * cols] = stacked[g * count : (g + 1) * count]
    rows = plain[...]
    pair = own.shape[0]
    half = pair // 2
    for steps, ref in enumerate((own, first, second, third)):
        section = order[steps]
        product[:, pl.ds(pl.multiple_of(section * pair, pair), pair)] = dot(rows, ref[...], 1)
    values = rows.astype(F32)
    squares = jnp.sum(values * values, axis=1, keepdims=True)
    lanes = lax.broadcasted_iota(jnp.int32, (count, pair), 1)
    sums[:, : 3 * pair] = product[:, : 3 * pair].astype(BF16)
    high, rest = rounded(squares)
    ends = jnp.where(lanes < half, product[:, 3 * pair :], high.astype(F32))
    sums[:, 3 * pair : 4 * pair] = jnp.where(lanes < half + half // 2, ends, rest).astype(BF16)
    for at in range(3):
        sums[:, (4 + at) * pair : (5 + at) * pair] = tiles[at * pair : (at + 1) * pair].astype(BF16)


def sections_kernel(
    features, order, s0, s1, s2, s3, plain, f0, f1, f2, f3, out, stack, expand, made, sent
):
    pair = f0.shape[0]
    rank = pair // 2
    count, width = plain.shape
    cols = width // GROUPS
    for steps, ref in enumerate((f0, f1, f2, f3)):
        section = order[steps]
        expand[pl.ds(pl.multiple_of(section * rank, rank), rank), :] = ref[rank:]

    def summed(at):
        columns = slice(at * pair, (at + 1) * pair)
        parts = [ref[:, columns].astype(F32) for ref in (s0, s1, s2, s3)]
        return (parts[0] + parts[1]) + (parts[2] + parts[3])

    y = [summed(s) for s in range(4)]
    square = y[3][:, rank : rank + 1] + y[3][:, pair - 1 :]
    stacks = [summed(4 + at) for at in range(3)]

    def thirds(place):
        at = (place % 2) * rank
        value = stacks[place // 2][at : at + rank]
        high, rest = rounded(value)
        middle, rest = rounded(rest)
        return jnp.concatenate([high, middle, rest.astype(BF16)], axis=0)

    uses = (((1, 0), (2, 1), (3, 3)), ((2, 2), (3, 4)), ((3, 5),))
    size = GROUPS * count
    moved = one_hot(block_places((1, size), 1, count), (size, size), 0)
    current = [plain[:, g * cols : (g + 1) * cols].astype(F32) for g in range(GROUPS)]
    sends = []
    for s in range(4):
        scale = lax.rsqrt(jnp.maximum(square, 0.0) / features + 1e-05)
        lower = (y[s][:, :rank] * scale).astype(BF16)
        if s < 3:
            added = dot(
                jnp.concatenate([lower] * 3, axis=1),
                jnp.concatenate([thirds(place) for _, place in uses[s]], axis=1),
            )
            value = lower.astype(F32)
            for at, (later, _) in enumerate(uses[s]):
                y[later] = y[later] + added[:, at * pair : (at + 1) * pair]
            ends = added[:, added.shape[1] - rank :]
            square = square + jnp.sum(
                value * (2.0 * y[s][:, rank:] + ends), axis=1, keepdims=True
            )
        for g in range(GROUPS):
            columns = slice(g * cols, (g + 1) * cols)
            current[g] = current[g] + dot(lower, expand[s * rank : (s + 1) * rank, columns])
            stack[s, g * count : (g + 1) * count] = current[g].astype(BF16)
        made[s] = dot(moved, stack[s]).astype(BF16)
        sends.append(
            pltpu.make_async_copy(made.at[s], out.at[pl.ds(s * size, size)], sent.at[s])
        )
        sends[-1].start()
    for copy in sends:
        copy.wait()


def unpack_kernel(places, back, out, made, sent):
    size, cols = places.shape[0], back.shape[2]
    count = size // GROUPS
    part = GROUPS * cols
    chosen = one_hot(places[...], (size, back.shape[1]), 1)
    sends = []
    for plane in range(back.shape[0]):
        found = dot(chosen, back[plane]).astype(BF16)
        for g in range(GROUPS):
            made[plane, :, g * cols : (g + 1) * cols] = found[g * count : (g + 1) * count]
        sends.append(
            pltpu.make_async_copy(
                made.at[plane], out.at[:, pl.ds(plane * part, part)], sent.at[plane]
            )
        )
        sends[-1].start()
    for copy in sends:
        copy.wait()


def local(hidden_in, request_adapter, home_slot, gains, shrink_tiles, expand_tiles):
    chips = lax.axis_size("chip")
    peers = 2 * chips
    sections = lax.axis_size("segment")
    plane = lax.axis_index("segment")
    core = lax.axis_index("core")
    count, width = hidden_in.shape
    part = width // sections
    cols = part // GROUPS
    total = home_slot.shape[0]
    rank = expand_tiles.shape[2]
    pair = 2 * rank
    depth = 2
    block = depth * GROUPS
    size = peers * block

    quarters = call(
        quarters_kernel,
        tuple(jax.ShapeDtypeStruct((pair, part), BF16) for _ in range(sections)),
        scratch=[
            pltpu.VMEM((sections, pair, part), BF16),
            pltpu.VMEM((1, width), F32),
            pltpu.SemaphoreType.DMA,
            pltpu.SemaphoreType.DMA((sections,)),
            pltpu.SemaphoreType.DMA((sections,)),
            pltpu.SemaphoreType.DMA((sections,)),
        ],
        out_spec=ANY,
        specs=[SMEM, ANY, ANY, ANY],
        room=60,
        name="quarters",
    )(plane.reshape(1), shrink_tiles[0, 0].T, gains, expand_tiles[0, 0])

    adapter_ids = request_adapter[:, 0]
    catalog = jnp.arange(total, dtype=jnp.int32)
    storage = jnp.sum(
        jnp.where(adapter_ids[:, None] == catalog[None, :], home_slot[None, :], 0), axis=1
    )
    order = jnp.arange(count, dtype=jnp.int32)
    same_adapter = adapter_ids[:, None] == adapter_ids[None, :]
    earlier = jnp.sum((same_adapter & (order[None, :] < order[:, None])).astype(jnp.int32), axis=1)
    groups = jnp.arange(GROUPS, dtype=jnp.int32)[:, None] * depth
    homes = (groups + (storage * block + earlier)[None, :]).reshape(-1)

    mine = lax.dynamic_slice(hidden_in, (0, plane * part), (count, part))
    packed = call(
        pack_kernel,
        jax.ShapeDtypeStruct((size, cols), BF16),
        specs=[VMEM, VMEM],
        name="pack",
    )(homes[None, :], mine)
    held = [quarters[0]] + [
        shifted(quarters[steps], "segment", steps) for steps in range(1, sections)
    ]

    arrived = lax.all_to_all(
        packed.reshape(chips, 2 * block, cols), "chip", split_axis=0, concat_axis=0, tiled=True
    )

    section_order = (plane - jnp.arange(sections, dtype=jnp.int32)) % sections
    section_order = jnp.concatenate([section_order, core.reshape(1)])
    tiles = call(
        factors_kernel,
        jax.ShapeDtypeStruct((6 * rank, pair), F32),
        scratch=[
            pltpu.VMEM((sections * pair, part), BF16),
            pltpu.VMEM((sections * rank, part), BF16),
        ],
        specs=[SMEM] + [VMEM] * 4,
        name="factors",
    )(section_order, *held)
    token = call(
        landed_kernel,
        jax.ShapeDtypeStruct((8, 128), F32),
        specs=[ANY] * 3,
        flops=LANDED_FLOPS,
        name="landed",
    )(*held[1:])
    arrived, token = lax.optimization_barrier((arrived, token))

    others = lax.ppermute(arrived, "core", [(0, 1), (1, 0)]).reshape(size, cols)
    sums, plain = call(
        products_kernel,
        (
            jax.ShapeDtypeStruct((peers * depth, 7 * pair), BF16),
            jax.ShapeDtypeStruct((peers * depth, part), BF16),
        ),
        scratch=[pltpu.VMEM((peers * depth, sections * pair), F32)],
        specs=[SMEM, ANY] + [VMEM] * 7,
        name="products",
    )(section_order, token, arrived.reshape(size, cols), others, tiles, *held)
    all_sums = [sums] + [shifted(sums, "segment", steps) for steps in range(1, sections)]

    results = call(
        lambda *refs: sections_kernel(width, *refs),
        jax.ShapeDtypeStruct((sections * size, cols), BF16),
        scratch=[
            pltpu.VMEM((sections, size, cols), BF16),
            pltpu.VMEM((sections * rank, part), BF16),
            pltpu.VMEM((sections, size, cols), BF16),
            pltpu.SemaphoreType.DMA((sections,)),
        ],
        specs=[SMEM] + [VMEM] * 9,
        out_spec=ANY,
        name="sections",
    )(section_order, *all_sums, plain, *held)

    back = lax.all_to_all(
        results.reshape(sections * peers, block, cols),
        ("segment", "chip", "core"),
        split_axis=0,
        concat_axis=0,
        tiled=True,
    )
    rows = call(
        unpack_kernel,
        jax.ShapeDtypeStruct((count, width), BF16),
        scratch=[
            pltpu.VMEM((sections, count, part), BF16),
            pltpu.SemaphoreType.DMA((sections,)),
        ],
        specs=[VMEM, VMEM],
        out_spec=ANY,
        name="unpack",
    )(homes[:, None], back.reshape(sections, size, cols))
    return rows[None]


def solution(mesh):
    planes, peers = mesh.devices.shape
    split = Mesh(mesh.devices.reshape(planes, peers // 2, 2), ("segment", "chip", "core"))
    rows = ("chip", "core")
    return jax.shard_map(
        local,
        mesh=split,
        in_specs=(
            P(rows, None),
            P(rows, None),
            P(),
            P("segment", None),
            P("segment", rows, None, None),
            P("segment", rows, None, None),
        ),
        out_specs=P("segment", rows, None),
        check_vma=False,
    )
```
